32 devices in a mesh: parts: 2 (over y), wide: 8 (over z, core), narrow: 2 (over x), sub: 1.
Axes of the slice: x: 2, y: 2, z: 4, core: 2. Of those that a mesh axis runs over, the one named last changes fastest.
Arguments:
- modes: float32 [128, 256, 512], P(('parts', 'wide'), None, ('narrow', 'sub')), parts along dimension 0, may hold values from -0.375 to 0.375
- eigvals: float32 [128, 512], P(('parts', 'wide'), ('narrow', 'sub')), parts along dimension 0, may hold values from 1 to 16
- stiff_tiles: float32 [128, 4, 2, 128, 256], P(('parts', 'wide'), 'narrow'), parts along dimension 0, may hold values from -0.18 to 0.18
- mass_tiles: float32 [128, 4, 2, 128, 256], P(('parts', 'wide'), 'narrow'), parts along dimension 0, may hold values from -0.18 to 0.18
- row_blocks: int32 [128, 4, 2], P(('parts', 'wide'), 'narrow'), parts along dimension 0, may hold values from 0 to 1
- adjacency: int32 [128, 4], P(('parts', 'wide')), parts along dimension 0, may hold values from 0 to 7, all different within a row; in each aligned block of 8 rows (0 to 7, 8 to 15, ...) at most 4 rows name the same one
- iface_stiff: float32 [16, 256, 256], P(('parts', 'wide'), ('narrow', 'sub')), parts along dimension 0, may hold values from -6 to 6
- iface_mass: float32 [16, 256, 256], P(('parts', 'wide'), ('narrow', 'sub')), parts along dimension 0, may hold values from -6 to 6
Outputs:
- reduced_stiff: float32 [16, 256, 256], P(('parts', 'wide'), ('narrow', 'sub')), parts along dimension 0
- reduced_mass: float32 [16, 256, 256], P(('parts', 'wide'), ('narrow', 'sub')), parts along dimension 0
The draws below stay inside these ranges and needn't reach their ends.
There are 2 independent parts, one for each index of `parts`. The reference program is written for one: setup_inputs(seed, part) draws one part's arguments, and reference() takes and returns one part's arrays. A program takes and returns all parts, laid end to end along the dimension named above; each array names one. Nothing has to cross between parts.
Inputs may be any that keep to these rules, and one draw needn't show every extreme that they name: `adjacency`: each row names 4 different interfaces. Within the rows of one index of wide (8 substructures in a row), no interface is named more than 4 times, a bound that some block reaches.
All inputs are finite; a program needn't handle non-finite values.
Results may differ from the reference program's by a relative error of at most 0.0001.
Values sent between devices are 32-bit elements; how exact they have to be, the bound alone decides.
No kernel may reach another device: no remote copies, remote signals or barrier semaphores. Data moves between devices by JAX's collectives and lax.ppermute only.
A program may use at most 128 MiB of HBM per device.

```python
import math
import jax
import jax.numpy as jnp
import numpy as np
from jax import lax

M = 512
C = 256
ROWT = 128
RB = 2
TPB = 2
ADJ = 4
SUB_W = 8
SUBS = 64
IFACES = 8
CAP = 4


def set_ends(values, key, low, largest):
    place = [jax.random.randint(jax.random.fold_in(key, axis), (), 0, length) for axis, length in enumerate(values.shape)]
    longest = values.shape.index(max(values.shape))
    neighbour = place[:longest] + [(place[longest] + 1) % values.shape[longest]] + place[longest + 1:]
    return values.at[tuple(place)].set(low).at[tuple(neighbour)].set(largest)


def levels(stream_key, shape, pieces, low, top_value):
    def one(dim, shards_of):
        steps = jax.random.uniform(jax.random.fold_in(jax.random.fold_in(stream_key, 6), dim), (shards_of,), jnp.float32, low / len(pieces), top_value / len(pieces))
        return jnp.repeat(jnp.exp(steps), shape[dim] // shards_of).reshape((-1,) + (1,) * (len(shape) - dim - 1))

    gain = one(*pieces[0])
    for cut in pieces[1:]:
        gain = gain * one(*cut)
    return gain


def deal_out(key, own, number, rows, count, top, limit, slope):
    ranking = jax.random.permutation(key, count)
    heavy_load, common = load_shares(count, rows * top, limit, slope, True), load_shares(count, rows * top, limit, slope, False)
    places = jnp.arange(count)

    def named(lengths, offset_by):
        used = int((lengths > 0).sum())
        fixed = max(1, used // 4)
        moved = fixed + (places - fixed + offset_by * (used - fixed)) % max(1, count - fixed)
        return jnp.zeros((count,), jnp.int32).at[ranking[jnp.where(places < fixed, places, moved)]].set(jnp.asarray(lengths, jnp.int32))

    lengths = jnp.where(number % 4 == 0, named(heavy_load, number // 4), named(common, number - number // 4 - 1))
    mixed = jax.random.permutation(jax.random.fold_in(own, 3), count)
    source_of, receiver = mixed[0:count // 2 * 2:2], mixed[1:count // 2 * 2:2]
    margin = jnp.minimum(lengths[source_of] - 1, limit - lengths[receiver]) // 2
    margin = jnp.where((source_of == ranking[0]) | (receiver == ranking[0]) | (lengths[receiver] == 0), 0, jnp.maximum(margin, 0))
    moved = jax.random.randint(jax.random.fold_in(own, 4), (count // 2,), 0, 1 << 20) % (margin + 1)
    lengths = lengths.at[source_of].add(-moved).at[receiver].add(moved)
    items = jnp.searchsorted(jnp.cumsum(lengths), jnp.arange(rows * top), side="right").astype(jnp.int32)
    grid = items.reshape(top, rows).T
    grid = grid[jax.random.permutation(jax.random.fold_in(own, 1), rows)]
    offset_by = jax.random.randint(jax.random.fold_in(own, 2), (rows, 1), 0, top)
    return jnp.take_along_axis(grid, (jnp.arange(top)[None, :] + offset_by) % top, axis=1)


def load_shares(amount, total, bound, slope, full):
    weights = [(1 << 20) // math.isqrt(rank ** slope) + 1 for rank in range(1, amount + 1)]
    largest = bound if full else min(bound, max(-(-total // amount), total * weights[0] // sum(weights)))
    least = 1 if total - largest >= amount - 1 else 0
    counts, rest = [largest] + [least] * (amount - 1), total - largest - least * (amount - 1)
    while rest > 0:
        candidates = [i for i in range(1, amount) if counts[i] < largest] or [i for i in range(1, amount) if counts[i] < bound]
        pool, budget = sum([weights[i] for i in candidates]), rest
        for i in candidates:
            more = min(bound - counts[i], max(1, budget * weights[i] // pool), rest)
            counts[i] = counts[i] + more
            rest = rest - more
    return np.array(counts)


def normal_values(stream_key, extent, spread, reach, shards=(), dtype=jnp.bfloat16):
    factor_of = levels(stream_key, extent, shards, -0.22, 0.18) if shards else 1.0
    drawn = jax.random.normal(stream_key, extent, jnp.float32) * spread * factor_of
    return jnp.minimum(jnp.maximum(drawn, -reach), reach).astype(dtype)


def setup_inputs(seed: int = 0, part: int = 0) -> dict:
    splits = jax.random.split(jax.random.key(seed), 9)
    own_keys = jax.random.split(jax.random.fold_in(splits[8], part), 9)
    modes = normal_values(own_keys[0], (SUBS, RB * ROWT, M), (TPB * ROWT) ** -0.5, 0.375, ((0, 8), (2, 2)), jnp.float32)
    eigvals = jnp.clip(jnp.exp(math.log(16.0) - 2.7725887 * jax.random.uniform(own_keys[1], (SUBS, M), jnp.float32) ** levels(own_keys[1], (SUBS, M), ((0, 8), (1, 2)), -0.2, 0.2)), 1.0, 16.0)
    stiff_tiles = normal_values(own_keys[2], (SUBS, ADJ, TPB, ROWT, C), 0.03, 0.18, ((0, 8), (1, 2)), jnp.float32)
    mass_tiles = normal_values(own_keys[3], (SUBS, ADJ, TPB, ROWT, C), 0.03, 0.18, ((0, 8), (1, 2)), jnp.float32)
    row_blocks = set_ends(jax.random.randint(own_keys[4], (SUBS, ADJ, TPB), 0, RB), jax.random.fold_in(own_keys[4], 1), 0, RB - 1).astype(jnp.int32)
    adjacency_keys = jax.random.split(jax.random.fold_in(own_keys[5], 1), SUBS // SUB_W)
    adjacency_turns = jax.random.permutation(jax.random.fold_in(own_keys[5], 3), SUBS // SUB_W)
    adjacency = jax.vmap(lambda own, number: deal_out(jax.random.fold_in(own_keys[5], 2), own, number, SUB_W, IFACES, ADJ, CAP, 2))(adjacency_keys, adjacency_turns).reshape((SUBS, ADJ))
    iface_stiff = normal_values(own_keys[6], (IFACES, C, C), 1.0, 6.0, ((0, 8), (1, 2)), jnp.float32)
    iface_mass = normal_values(own_keys[7], (IFACES, C, C), 1.0, 6.0, ((0, 8), (1, 2)), jnp.float32)
    return {"modes": modes, "eigvals": eigvals, "stiff_tiles": stiff_tiles, "mass_tiles": mass_tiles, "row_blocks": row_blocks, "adjacency": adjacency, "iface_stiff": iface_stiff, "iface_mass": iface_mass}


def reference(modes, eigvals, stiff_tiles, mass_tiles, row_blocks, adjacency, iface_stiff, iface_mass):
    highest = lax.Precision.HIGHEST
    inverse = 1.0 / eigvals

    def per_substructure(carry, inputs):
        acc_stiff, acc_mass = carry
        modal, inv_row, stiff, mass, blocks, owners = inputs
        tiled = modal.reshape(RB, ROWT, M)
        chosen = tiled[blocks]
        proj_stiff = jnp.einsum("jtrm,jtrc->jmc", chosen, stiff, precision=highest)
        proj_mass = jnp.einsum("jtrm,jtrc->jmc", chosen, mass, precision=highest)
        weight_one = inv_row[None, :, None]
        part_stiff = jnp.einsum("jmc,jmd->jcd", proj_stiff, weight_one * proj_stiff, precision=highest)
        cross = jnp.einsum("jmc,jmd->jcd", proj_stiff, weight_one * proj_mass, precision=highest)
        second = jnp.einsum("jmc,jmd->jcd", proj_stiff, weight_one * weight_one * proj_stiff, precision=highest)
        part_mass = second - cross - jnp.swapaxes(cross, 1, 2)
        acc_stiff = acc_stiff.at[owners].add(part_stiff)
        acc_mass = acc_mass.at[owners].add(part_mass)
        return (acc_stiff, acc_mass), None

    start = (jnp.zeros((IFACES, C, C), jnp.float32), jnp.zeros((IFACES, C, C), jnp.float32))
    (sum_stiff, sum_mass), _ = lax.scan(per_substructure, start, (modes, inverse, stiff_tiles, mass_tiles, row_blocks, adjacency))
    return iface_stiff - sum_stiff, iface_mass + sum_mass
```

```python
import functools

import jax
import jax.numpy as jnp
from jax import lax
from jax.experimental import pallas as pl
from jax.experimental.pallas import tpu as pltpu
from jax.sharding import PartitionSpec as P

ROWT = 128
LANES = 128
GROUP = 8
FIRST = 4
LAST = 1
VMEM_LIMIT = 56 * 1024 * 1024

f32 = jnp.float32
bf16 = jnp.bfloat16


def split(x):
    high = x.astype(bf16)
    return high, (x - high.astype(f32)).astype(bf16)


def product(a, b, a_dim, b_dim):
    def one(x, y):
        return lax.dot_general(
            x, y, (((a_dim,), (b_dim,)), ((), ())), preferred_element_type=f32
        )

    return one(a[0], b[0]) + (one(a[0], b[1]) + one(a[1], b[0]))


def stacked(a, b, axis):
    return tuple(jnp.concatenate(pair, axis) for pair in zip(a, b, strict=True))


def full_rows(tiles_ref, slot, blocks_ref, sub, row_tiles):
    tiles = tiles_ref.shape[2]
    rows = []
    for r in range(row_tiles):
        total = None
        for t in range(tiles):
            here = (blocks_ref[sub, slot, t] == r).astype(f32)
            term = tiles_ref[0, slot, t] * here
            total = term if total is None else total + term
        rows.append(total)
    return jnp.concatenate(rows, 0)


def add_substructure(
    sub, mode_refs, eig_refs, stiff_ref, mass_ref, blocks_ref, adjacency_ref, first_slot, acc_ref
):
    gram = None
    for modes_ref, eig_ref in zip(mode_refs, eig_refs, strict=True):
        phi = modes_ref[...]
        inverse = 1.0 / eig_ref[pl.ds(sub, 1), :]
        once = phi * inverse
        twice = once * inverse
        term = product(stacked(split(once), split(twice), 0), split(phi), 1, 1)
        gram = term if gram is None else gram + term
    rows = gram.shape[1]
    gram = split(jnp.concatenate([gram[:rows], 0.5 * gram[rows:]], 0))
    gram_one = (gram[0][:rows], gram[1][:rows])
    for slot in range(stiff_ref.shape[1]):
        stiff = split(full_rows(stiff_ref, slot, blocks_ref, sub, rows // ROWT))
        mass = split(full_rows(mass_ref, slot, blocks_ref, sub, rows // ROWT))
        both = product(gram, stiff, 1, 0)
        cross = product(gram_one, mass, 1, 0)
        right = stacked(split(both[:rows]), split(both[rows:] - cross), 1)
        owner = adjacency_ref[sub, first_slot + slot]
        acc_ref[owner] += product(stiff, right, 0, 0)


def sum_kernel(n_parts, start, has_acc, info, blocks, adjacency, *refs):
    mode_refs, eig_refs = refs[:n_parts], refs[n_parts : 2 * n_parts]
    stiff_ref, mass_ref = refs[2 * n_parts : 2 * n_parts + 2]
    acc_in = refs[2 * n_parts + 2] if has_acc else None
    acc_ref = refs[-1]

    @pl.when(pl.program_id(0) == 0)
    def _():
        acc_ref[...] = acc_in[...] if has_acc else jnp.zeros_like(acc_ref)

    add_substructure(
        pl.program_id(0) + start,
        mode_refs,
        eig_refs,
        stiff_ref,
        mass_ref,
        blocks,
        adjacency,
        info[0] * stiff_ref.shape[1],
        acc_ref,
    )


def pack_interface(acc_ref, owner, out_ref, place):
    half = ROWT // 2
    row = lax.broadcasted_iota(jnp.int32, (ROWT, ROWT), 0)
    col = lax.broadcasted_iota(jnp.int32, (ROWT, ROWT), 1)
    low, mid = slice(0, ROWT), slice(ROWT, 2 * ROWT)
    diagonals = []
    for which in range(2):
        base = which * 2 * ROWT
        lanes_low, lanes_mid = slice(base, base + ROWT), slice(base + ROWT, base + 2 * ROWT)
        first, second = acc_ref[owner, low, lanes_low], acc_ref[owner, mid, lanes_mid]
        corner = acc_ref[owner, mid, lanes_low]
        square = jnp.where(row > col, first, second)
        diagonal = jnp.sum(jnp.where(row == col, first, 0.0), axis=0, keepdims=True)
        if which == 1:
            corner = corner + acc_ref[owner, low, lanes_mid].T
            square = square + jnp.where(row < col, first, second).T
            diagonal = diagonal + diagonal
        diagonals.append(diagonal)
        for part in range(2):
            rows = slice(part * half, (part + 1) * half)
            out_ref[part, place, which * half : (which + 1) * half, :LANES] = corner[rows]
            out_ref[part, place, which * half : (which + 1) * half, LANES:] = square[rows]
    extra = jnp.broadcast_to(jnp.concatenate(diagonals, 1), (GROUP, 2 * LANES))
    for part in range(2):
        out_ref[part, place, 2 * half :, :] = extra


def last_kernel(n_parts, start, count, info, blocks, adjacency, *refs):
    mode_refs, eig_refs = refs[:n_parts], refs[n_parts : 2 * n_parts]
    stiff_ref, mass_ref, acc_in, send_ref, keep_ref, acc_ref = refs[2 * n_parts :]

    @pl.when(pl.program_id(0) == 0)
    def _():
        acc_ref[...] = acc_in[...]

    add_substructure(
        pl.program_id(0) + start,
        mode_refs,
        eig_refs,
        stiff_ref,
        mass_ref,
        blocks,
        adjacency,
        info[0] * stiff_ref.shape[1],
        acc_ref,
    )

    @pl.when(pl.program_id(0) == count - 1)
    def _():
        chips = send_ref.shape[1]
        chip, core = info[1], info[2]
        for shift in range(chips):
            target = lax.rem(chip + shift, chips) * 2
            pack_interface(acc_ref, target + 1 - core, send_ref, shift)
            pack_interface(acc_ref, target + core, keep_ref, shift)


def sums_of(info, blocks, adjacency, parts, eigs, stiff, mass, start, count, ifaces, acc=None, chips=0):
    subs, slots, tiles, rowt, width = stiff.shape
    n_parts = len(parts)
    rows = parts[0][2]
    scalars = pl.BlockSpec(memory_space=pltpu.SMEM)
    in_specs = [scalars] * 3
    operands = [info, blocks, adjacency]
    for array, first, height in parts:
        in_specs.append(
            pl.BlockSpec(
                (height, array.shape[1]), functools.partial(lambda o, i: (i + o, 0), start - first)
            )
        )
        operands.append(array)
    for array, place in eigs:
        in_specs.append(
            pl.BlockSpec((subs, array.shape[1]), functools.partial(lambda o, i: (o, 0), place))
        )
        operands.append(array)
    for array in (stiff, mass):
        in_specs.append(
            pl.BlockSpec((1, slots, tiles, rowt, width), lambda i: (i + start, 0, 0, 0, 0))
        )
        operands.append(array)
    acc_shape = (ifaces, width, 2 * width)
    if acc is not None:
        in_specs.append(
            pl.BlockSpec(acc_shape, lambda i: (0, 0, 0), pipeline_mode=pl.Buffered(1))
        )
        operands.append(acc)
    if chips:
        kernel = functools.partial(last_kernel, n_parts, start, count)
        packed = (2, chips, ROWT + GROUP, 2 * LANES)
        out_shape = (jax.ShapeDtypeStruct(packed, f32),) * 2
        out_specs = (pl.BlockSpec(packed, lambda i: (0, 0, 0, 0)),) * 2
        scratch = [pltpu.VMEM(acc_shape, f32)]
    else:
        kernel = functools.partial(sum_kernel, n_parts, start, acc is not None)
        out_shape = jax.ShapeDtypeStruct(acc_shape, f32)
        out_specs = pl.BlockSpec(acc_shape, lambda i: (0, 0, 0))
        scratch = []
    modes_held = sum(array.shape[1] for array, _, _ in parts)
    flops = 6 * count * (2 * rows * rows * modes_held + 5 * slots * rows * rows * width)
    moved = 4 * (count * (rows * modes_held + 2 * slots * tiles * rowt * width))
    moved = moved + 8 * ifaces * width * 2 * width
    return pl.pallas_call(
        kernel,
        grid=(count,),
        in_specs=in_specs,
        out_specs=out_specs,
        out_shape=out_shape,
        scratch_shapes=scratch,
        compiler_params=pltpu.CompilerParams(vmem_limit_bytes=VMEM_LIMIT),
        cost_estimate=pl.CostEstimate(flops=flops, bytes_accessed=moved, transcendentals=0),
    )(*operands)


def unpack_kernel(info, mine, theirs, stiff_ref, mass_ref, out_stiff, out_mass):
    half = ROWT // 2
    side = info[0]
    row = lax.broadcasted_iota(jnp.int32, (ROWT, ROWT), 0)
    col = lax.broadcasted_iota(jnp.int32, (ROWT, ROWT), 1)
    a, b = mine[...], theirs[...]
    upper = jnp.where(side == 0, a, b)
    lower = jnp.where(side == 0, b, a)
    for which, (iface_ref, out_ref) in enumerate(((stiff_ref, out_stiff), (mass_ref, out_mass))):
        sign = -1.0 if which == 0 else 1.0
        rows = slice(which * half, (which + 1) * half)
        packed = jnp.concatenate([upper[rows], lower[rows]], 0)
        corner, square = packed[:, :LANES], packed[:, LANES:]
        diagonal = upper[2 * half : 2 * half + 1, which * LANES : (which + 1) * LANES]
        flipped = square.T

        @pl.when(side == 0)
        def _():
            first = jnp.where(row > col, square, jnp.where(row == col, diagonal, flipped))
            out_ref[0, :, :LANES] = iface_ref[0, :, :LANES] + sign * first
            out_ref[0, :, LANES:] = iface_ref[0, :, LANES:] + sign * corner.T

        @pl.when(side != 0)
        def _():
            second = jnp.where(row <= col, square, flipped)
            out_ref[0, :, :LANES] = iface_ref[0, :, :LANES] + sign * corner
            out_ref[0, :, LANES:] = iface_ref[0, :, LANES:] + sign * second


def unpack(info, mine, theirs, iface_stiff, iface_mass):
    scalars = pl.BlockSpec(memory_space=pltpu.SMEM)
    whole = pl.BlockSpec(memory_space=pltpu.VMEM)
    return pl.pallas_call(
        unpack_kernel,
        in_specs=[scalars] + [whole] * 4,
        out_specs=(whole, whole),
        out_shape=(jax.ShapeDtypeStruct(iface_stiff.shape, f32),) * 2,
        compiler_params=pltpu.CompilerParams(vmem_limit_bytes=VMEM_LIMIT),
    )(info, mine, theirs, iface_stiff, iface_mass)


def paired(modes, eigvals, stiff, mass, blocks, adjacency, iface_stiff, iface_mass):
    subs, rows, held = modes.shape
    n_wide = lax.axis_size("wide")
    chips = n_wide // 2
    side, wide = lax.axis_index("narrow"), lax.axis_index("wide")
    info = jnp.stack([side, wide // 2, wide % 2]).astype(jnp.int32)
    flat = modes.reshape(subs * rows, held)
    swap = [(0, 1), (1, 0)]

    last = min(LAST, subs - 1)
    first = min(FIRST, subs - last)
    cuts = sorted({0, first, subs - last, subs})
    arrived = []
    for begin, end in zip(cuts[:-1], cuts[1:], strict=True):
        piece = flat[begin * rows : end * rows]
        if begin == 0:
            piece = jnp.concatenate([piece, eigvals], 0)
        else:
            piece, _ = lax.optimization_barrier((piece, arrived[-1][0]))
        arrived.append((lax.ppermute(piece, "narrow", swap), begin, end))
    eigs = [(eigvals, 0), (arrived[0][0], first * rows // subs)]
    acc = None
    for piece, begin, end in arrived:
        acc = sums_of(
            info,
            blocks,
            adjacency,
            [(flat, 0, rows), (piece, begin, rows)],
            eigs,
            stiff,
            mass,
            begin,
            end - begin,
            n_wide,
            acc,
            chips if end == subs else 0,
        )
    send, keep = acc

    def other(x, i):
        return lax.dynamic_index_in_dim(x, i, 0, keepdims=False)

    got = lax.ppermute(send, "wide", [(i, i ^ 1) for i in range(n_wide)])
    away = other(keep, 1 - side) + other(got, 1 - side)
    came = lax.ppermute(away, "narrow", swap)
    here = other(keep, side) + other(got, side)
    total = here[0] + came[0]
    for shift in range(1, chips):
        ring = [(i, (i + 2 * shift) % n_wide) for i in range(n_wide)]
        total = total + lax.ppermute(here[shift] + came[shift], "wide", ring)
    return unpack(info, total, lax.ppermute(total, "narrow", swap), iface_stiff, iface_mass)


def grouped(modes, eigvals, stiff, mass, blocks, adjacency, iface_stiff, iface_mass):
    subs, rows, _ = modes.shape
    width = stiff.shape[4]
    n_wide = lax.axis_size("wide")
    info = jnp.stack([lax.axis_index("narrow")] * 3).astype(jnp.int32)
    modes = lax.all_gather(modes, "narrow", axis=2, tiled=True)
    eigvals = lax.all_gather(eigvals, "narrow", axis=1, tiled=True)
    flat = modes.reshape(subs * rows, modes.shape[2])
    acc = sums_of(
        info, blocks, adjacency, [(flat, 0, rows)], [(eigvals, 0)], stiff, mass, 0, subs, n_wide
    )
    half = acc[:, :, width:]
    part = jnp.concatenate([acc[:, :, :width], half + jnp.swapaxes(half, 1, 2)], 2)
    part = lax.psum_scatter(part, "wide", scatter_dimension=0, tiled=True)
    part = lax.psum_scatter(part, ("narrow", "sub"), scatter_dimension=1, tiled=True)
    return iface_stiff - part[:, :, :width], iface_mass + part[:, :, width:]


def solution(mesh):
    pairs = mesh.shape["narrow"] == 2 and mesh.shape["sub"] == 1 and mesh.shape["wide"] % 2 == 0
    return jax.shard_map(
        paired if pairs else grouped,
        mesh=mesh,
        in_specs=(
            P(("parts", "wide"), None, ("narrow", "sub")),
            P(("parts", "wide"), ("narrow", "sub")),
            P(("parts", "wide"), "narrow", None, None, None),
            P(("parts", "wide"), "narrow", None, None, None),
            P(("parts", "wide"), "narrow", None),
            P(("parts", "wide"), None),
            P(("parts", "wide"), ("narrow", "sub"), None),
            P(("parts", "wide"), ("narrow", "sub"), None),
        ),
        out_specs=(
            P(("parts", "wide"), ("narrow", "sub"), None),
            P(("parts", "wide"), ("narrow", "sub"), None),
        ),
        check_vma=False,
    )
```

```python
import functools

import jax
import jax.numpy as jnp
from jax import lax
from jax.experimental import pallas as pl
from jax.experimental.pallas import tpu as pltpu
from jax.sharding import PartitionSpec as P

ROWT = 128
LANES = 128
GROUP = 8
PIECE = (2 * ROWT + GROUP) // 3
MIB = 1024 * 1024

f32 = jnp.float32
bf16 = jnp.bfloat16


def split(x):
    high = x.astype(bf16)
    return high, (x - high.astype(f32)).astype(bf16)


def left(pair, axis):
    return jnp.concatenate([pair[0], pair[1], pair[0]], axis)


def right(pair, axis):
    return jnp.concatenate([pair[0], pair[0], pair[1]], axis)


def product(a, b, a_dim, b_dim):
    return lax.dot_general(a, b, (((a_dim,), (b_dim,)), ((), ())), preferred_element_type=f32)


def full_rows(tiles_ref, slot, blocks_ref, sub, row_tiles):
    tiles = tiles_ref.shape[2]
    rows = []
    for r in range(row_tiles):
        total = None
        for t in range(tiles):
            here = (blocks_ref[sub, slot, t] == r).astype(f32)
            term = tiles_ref[0, slot, t] * here
            total = term if total is None else total + term
        rows.append(total)
    return jnp.concatenate(rows, 0)


def contributions(phi, inverse, stiffs, masses):
    held = phi.shape[1]
    width = stiffs[0][0].shape[1]
    sides = [jnp.concatenate(x, 1) for x in zip(*stiffs, *masses, strict=True)]
    projected = product(left(split(phi.T), 1), right(sides, 0), 1, 0)
    scale = jnp.broadcast_to(inverse, (LANES, held)).T
    scale = jnp.concatenate([scale] * (width // LANES), 1)
    slots = len(stiffs)
    for slot in range(slots):
        p = projected[:, slot * width : (slot + 1) * width]
        q = projected[:, (slots + slot) * width : (slots + slot + 1) * width]
        first = scale * p
        second = scale * (0.5 * first - q)
        both = [jnp.concatenate(x, 1) for x in zip(split(first), split(second), strict=True)]
        yield product(left(split(p.T), 1), right(both, 0), 1, 0)


def local_kernel(start, has_acc, info, blocks, adjacency, modes_ref, eig_ref, stiff_ref, mass_ref, *refs):
    acc_in = refs[0] if has_acc else None
    s_ref, m_ref, acc_ref = refs[-3:]

    @pl.when(pl.program_id(0) == 0)
    def _():
        acc_ref[...] = acc_in[...] if has_acc else jnp.zeros_like(acc_ref)

    sub = pl.program_id(0) + start
    row_tiles = modes_ref.shape[0] // ROWT
    slots = stiff_ref.shape[1]
    stiffs, masses = [], []
    for slot in range(slots):
        for pairs, tiles_ref, pair_ref in ((stiffs, stiff_ref, s_ref), (masses, mass_ref, m_ref)):
            pairs.append(split(full_rows(tiles_ref, slot, blocks, sub, row_tiles)))
            pair_ref[0, slot, 0], pair_ref[0, slot, 1] = pairs[-1]
    inverse = 1.0 / eig_ref[pl.ds(sub, 1), :]
    for slot, update in enumerate(contributions(modes_ref[...], inverse, stiffs, masses)):
        acc_ref[adjacency[sub, info[0] * slots + slot]] += update


def whole(shape):
    return pl.BlockSpec(shape, functools.partial(lambda n, i: (0,) * n, len(shape)))


def once(shape):
    return pl.BlockSpec(
        shape, functools.partial(lambda n, i: (0,) * n, len(shape)), pipeline_mode=pl.Buffered(1)
    )


def params(limit):
    return pltpu.CompilerParams(vmem_limit_bytes=limit * MIB)


def cost(count, rows, held, slots, width):
    flops = 6 * count * 4 * slots * rows * held * width
    return pl.CostEstimate(flops=flops, bytes_accessed=count * 3 * MIB, transcendentals=0)


def local_sums(scalars, flat, eigvals, stiff, mass, start, count, limit, ifaces, acc=None):
    subs, slots, tiles, rowt, width = stiff.shape
    held = flat.shape[1]
    rows = flat.shape[0] // subs
    tile_spec = pl.BlockSpec((1, slots, tiles, rowt, width), lambda i: (i + start, 0, 0, 0, 0))
    pair_spec = pl.BlockSpec((1, slots, 2, rows, width), lambda i: (i, 0, 0, 0, 0))
    pair = jax.ShapeDtypeStruct((count, slots, 2, rows, width), bf16)
    shape = (ifaces, width, 2 * width)
    given = [] if acc is None else [acc]
    return pl.pallas_call(
        functools.partial(local_kernel, start, acc is not None),
        grid=(count,),
        in_specs=[pl.BlockSpec(memory_space=pltpu.SMEM)] * 3
        + [pl.BlockSpec((rows, held), lambda i: (i + start, 0)), whole(eigvals.shape), tile_spec, tile_spec]
        + [once(shape)] * len(given),
        out_specs=[pair_spec, pair_spec, whole(shape)],
        out_shape=[pair, pair, jax.ShapeDtypeStruct(shape, f32)],
        compiler_params=params(limit),
        cost_estimate=cost(count, rows, held, slots, width),
    )(*scalars, flat, eigvals, stiff, mass, *given)


def pairs_of(ref, place=0):
    return [(ref[place, slot, 0], ref[place, slot, 1]) for slot in range(ref.shape[1])]


def sum_kernel(start, info, adjacency, modes_ref, eig_ref, s_ref, m_ref, acc_in, acc_ref):
    @pl.when(pl.program_id(0) == 0)
    def _():
        acc_ref[...] = acc_in[...]

    sub = pl.program_id(0) + start
    slots = s_ref.shape[1]
    inverse = 1.0 / eig_ref[pl.ds(sub, 1), :]
    sums = contributions(modes_ref[...], inverse, pairs_of(s_ref), pairs_of(m_ref))
    for slot, update in enumerate(sums):
        acc_ref[adjacency[sub, info[0] * slots + slot]] += update


def pair_specs(pairs, offset):
    return [
        pl.BlockSpec((1, *pair.shape[1:]), lambda i: (i + offset, 0, 0, 0, 0)) for pair in pairs
    ]


def arrived_sums(scalars, modes, eigs, pairs, start, offset, count, acc):
    slots, _, rows, width = pairs[0].shape[1:]
    held = modes.shape[1]
    return pl.pallas_call(
        functools.partial(sum_kernel, start),
        grid=(count,),
        in_specs=[pl.BlockSpec(memory_space=pltpu.SMEM)] * 2
        + [pl.BlockSpec((rows, held), lambda i: (i, 0)), whole(eigs.shape)]
        + pair_specs(pairs, offset)
        + [once(acc.shape)],
        out_specs=whole(acc.shape),
        out_shape=jax.ShapeDtypeStruct(acc.shape, f32),
        compiler_params=params(24),
        cost_estimate=cost(count, rows, held, slots, width),
    )(*scalars, modes, eigs, *pairs, acc)


def pack(sums):
    row = lax.broadcasted_iota(jnp.int32, (ROWT, ROWT), 0)
    col = lax.broadcasted_iota(jnp.int32, (ROWT, ROWT), 1)
    packed, diagonals = [], []
    for which in range(2):
        base = which * 2 * ROWT
        first = sums(slice(0, ROWT), slice(base, base + ROWT))
        second = sums(slice(ROWT, 2 * ROWT), slice(base + ROWT, base + 2 * ROWT))
        corner = sums(slice(ROWT, 2 * ROWT), slice(base, base + ROWT))
        square = jnp.where(row > col, first, second)
        diagonal = jnp.sum(jnp.where(row == col, first, 0.0), axis=0, keepdims=True)
        if which == 1:
            corner = corner + sums(slice(0, ROWT), slice(base + ROWT, base + 2 * ROWT)).T
            square = square + jnp.where(row < col, first, second).T
            diagonal = diagonal + diagonal
        packed.append(jnp.concatenate([corner, square], 1))
        diagonals.append(diagonal)
    packed.append(jnp.broadcast_to(jnp.concatenate(diagonals, 1), (GROUP, 2 * LANES)))
    return jnp.concatenate(packed, 0)


def places(side):
    return ((0, 0), (1, 2 - side), (2, 1 + side))


def pack_kernel(info, acc_ref, send_ref, keep_ref):
    side, chip, core = info[0], info[1], info[2]

    def one(shift, carry):
        target = lax.bitwise_xor(chip, shift) * 2
        for owner, out_ref in ((target + 1 - core, send_ref), (target + core, keep_ref)):
            packed = pack(lambda r, c, o=owner: acc_ref[o, r, c])
            for piece, place in places(side):
                out_ref[place, shift] = packed[piece * PIECE : (piece + 1) * PIECE]
        return carry

    lax.fori_loop(0, send_ref.shape[1], one, 0)


def packed_sums(info, acc, shape):
    return pl.pallas_call(
        pack_kernel,
        in_specs=[pl.BlockSpec(memory_space=pltpu.SMEM), pl.BlockSpec(memory_space=pltpu.VMEM)],
        out_specs=[pl.BlockSpec(memory_space=pltpu.VMEM)] * 2,
        out_shape=[jax.ShapeDtypeStruct(shape, f32)] * 2,
        compiler_params=params(16),
        cost_estimate=pl.CostEstimate(flops=8_000_000, bytes_accessed=MIB, transcendentals=0),
    )(info, acc)


def add_kernel(
    sub, info, adjacency, modes_ref, eig_ref, s_ref, m_ref, send_in, keep_in, send_ref, keep_ref, held, sems
):
    side, chip, core = info[0], info[1], info[2]
    slots = s_ref.shape[1]

    def copies(slot, inward):
        owner = adjacency[sub, side * slots + slot]
        shift = lax.bitwise_xor(owner // 2, chip)
        mine = lax.rem(owner, 2) == core
        for here, ref in ((mine, keep_ref), (jnp.logical_not(mine), send_ref)):
            ends = (ref.at[:, shift], held.at[slot])
            source, target = ends if inward else ends[::-1]
            yield here, pltpu.make_async_copy(source, target, sems.at[slot])

    def run(slot, inward, wait):
        for here, copy in copies(slot, inward):

            @pl.when(here)
            def _(copy=copy):
                if wait:
                    copy.wait()
                else:
                    copy.start()

    for slot in range(slots):
        run(slot, True, False)
    inverse = 1.0 / eig_ref[sub : sub + 1, :]
    sums = contributions(modes_ref[...], inverse, pairs_of(s_ref), pairs_of(m_ref))
    for slot, update in enumerate(sums):
        packed = pack(lambda r, c, u=update: u[r, c])
        run(slot, True, True)
        for piece, place in places(side):
            held[slot, place] += packed[piece * PIECE : (piece + 1) * PIECE]
        run(slot, False, False)
    for slot in range(slots):
        run(slot, False, True)


def added_sums(scalars, modes, eigs, pairs, sub, offset, sums):
    slots, _, rows, width = pairs[0].shape[1:]
    held = modes.shape[1]
    anywhere = pl.BlockSpec(memory_space=pl.ANY)
    _, _, *piece = sums[0].shape
    return pl.pallas_call(
        functools.partial(add_kernel, sub),
        grid=(1,),
        in_specs=[pl.BlockSpec(memory_space=pltpu.SMEM)] * 2
        + [pl.BlockSpec((rows, held), lambda i: (i, 0)), whole(eigs.shape)]
        + pair_specs(pairs, offset)
        + [anywhere] * 2,
        out_specs=[anywhere] * 2,
        out_shape=[jax.ShapeDtypeStruct(x.shape, f32) for x in sums],
        scratch_shapes=[
            pltpu.VMEM((slots, sums[0].shape[0], *piece), f32),
            pltpu.SemaphoreType.DMA((slots,)),
        ],
        input_output_aliases={6: 0, 7: 1},
        compiler_params=params(16),
        cost_estimate=cost(1, rows, held, slots, width),
    )(*scalars, modes, eigs, *pairs, *sums)


def unpack_kernel(info, early_mine, early_theirs, mine, theirs, stiff_ref, mass_ref, out_stiff, out_mass):
    side = info[0]
    row = lax.broadcasted_iota(jnp.int32, (ROWT, ROWT), 0)
    col = lax.broadcasted_iota(jnp.int32, (ROWT, ROWT), 1)
    a, b = mine[...], theirs[...]
    packed = jnp.concatenate(
        [early_mine[...] + early_theirs[...], jnp.where(side == 0, a, b), jnp.where(side == 0, b, a)], 0
    )
    for which, (iface_ref, out_ref) in enumerate(((stiff_ref, out_stiff), (mass_ref, out_mass))):
        sign = -1.0 if which == 0 else 1.0
        rows = packed[which * ROWT : (which + 1) * ROWT]
        corner, square = rows[:, :LANES], rows[:, LANES:]
        diagonal = packed[2 * ROWT : 2 * ROWT + 1, which * LANES : (which + 1) * LANES]
        flipped = square.T

        @pl.when(side == 0)
        def _():
            first = jnp.where(row > col, square, jnp.where(row == col, diagonal, flipped))
            out_ref[0, :, :LANES] = iface_ref[0, :, :LANES] + sign * first
            out_ref[0, :, LANES:] = iface_ref[0, :, LANES:] + sign * corner.T

        @pl.when(side != 0)
        def _():
            second = jnp.where(row <= col, square, flipped)
            out_ref[0, :, :LANES] = iface_ref[0, :, :LANES] + sign * corner
            out_ref[0, :, LANES:] = iface_ref[0, :, LANES:] + sign * second


def unpack(info, sums, iface_stiff, iface_mass):
    vmem = pl.BlockSpec(memory_space=pltpu.VMEM)
    return pl.pallas_call(
        unpack_kernel,
        in_specs=[pl.BlockSpec(memory_space=pltpu.SMEM)] + [vmem] * 6,
        out_specs=(vmem, vmem),
        out_shape=(jax.ShapeDtypeStruct(iface_stiff.shape, f32),) * 2,
        compiler_params=params(8),
    )(info, *sums, iface_stiff, iface_mass)


def paired(modes, eigvals, stiff, mass, blocks, adjacency, iface_stiff, iface_mass):
    subs, rows, held = modes.shape
    n_wide = lax.axis_size("wide")
    chips = n_wide // 2
    side, wide = lax.axis_index("narrow"), lax.axis_index("wide")
    info = jnp.stack([side, wide // 2, wide % 2]).astype(jnp.int32)
    flat = modes.reshape(subs * rows, held)

    def swap(x):
        return lax.ppermute(x, "narrow", [(0, 1), (1, 0)])

    def over_wide(x, mask):
        return lax.ppermute(x, "wide", [(i, i ^ mask) for i in range(n_wide)])

    def after(x, *others):
        return lax.optimization_barrier((x, *others))

    half = subs // 2
    cuts = [0, half, subs - 2, subs - 1, subs]
    pieces = [flat[a * rows : b * rows] for a, b in zip(cuts[:-1], cuts[1:], strict=True)]
    came = [swap(pieces[0])]
    local = functools.partial(local_sums, [info, blocks, adjacency], flat, eigvals, stiff, mass)
    *early, acc = local(0, half, 28, n_wide)
    sent, acc = after(eigvals, acc)
    eigs = swap(sent)
    *late, acc = local(half, subs - half, 28, n_wide, acc)
    sent, acc = after(pieces[1], acc)
    came.append(swap(sent))
    sent, came[0] = after(pieces[2], came[0])
    came.append(swap(sent))

    scalars = [info, adjacency]
    acc = arrived_sums(scalars, came[0], eigs, early, 0, 0, half, acc)
    sent, acc = after(pieces[3], acc)
    came.append(swap(sent))
    acc = arrived_sums(scalars, came[1], eigs, late, half, 0, cuts[2] - half, acc)
    sums = packed_sums(info, acc, (3, chips, PIECE, 2 * LANES))
    for k in (2, 3):
        sums = added_sums(scalars, came[k], eigs, late, cuts[k], cuts[k] - half, sums)
    send, keep = sums

    def over_chips(x):
        total = x[0]
        for shift in range(1, chips):
            total = total + over_wide(x[shift], 2 * shift)
        return total

    got = over_wide(send, 1)
    away = swap(keep[1] + got[1])
    first = over_chips(keep[0] + got[0])
    first_theirs = swap(first)
    second = over_chips(keep[2] + got[2] + away)
    second_theirs = swap(second)
    return unpack(info, (first, first_theirs, second, second_theirs), iface_stiff, iface_mass)


def grouped(modes, eigvals, stiff, mass, blocks, adjacency, iface_stiff, iface_mass):
    subs, rows, _ = modes.shape
    width = stiff.shape[4]
    n_wide = lax.axis_size("wide")
    info = jnp.stack([lax.axis_index("narrow")] * 3).astype(jnp.int32)
    modes = lax.all_gather(modes, "narrow", axis=2, tiled=True)
    eigvals = lax.all_gather(eigvals, "narrow", axis=1, tiled=True)
    flat = modes.reshape(subs * rows, modes.shape[2])
    _, _, acc = local_sums([info, blocks, adjacency], flat, eigvals, stiff, mass, 0, subs, 52, n_wide)
    half = acc[:, :, width:]
    part = jnp.concatenate([acc[:, :, :width], half + jnp.swapaxes(half, 1, 2)], 2)
    part = lax.psum_scatter(part, "wide", scatter_dimension=0, tiled=True)
    part = lax.psum_scatter(part, ("narrow", "sub"), scatter_dimension=1, tiled=True)
    return iface_stiff - part[:, :, :width], iface_mass + part[:, :, width:]


def solution(mesh):
    wide = mesh.shape["wide"]
    pairs = mesh.shape["narrow"] == 2 and mesh.shape["sub"] == 1 and wide > 1 and wide & (wide - 1) == 0
    return jax.shard_map(
        paired if pairs else grouped,
        mesh=mesh,
        in_specs=(
            P(("parts", "wide"), None, ("narrow", "sub")),
            P(("parts", "wide"), ("narrow", "sub")),
            P(("parts", "wide"), "narrow", None, None, None),
            P(("parts", "wide"), "narrow", None, None, None),
            P(("parts", "wide"), "narrow", None),
            P(("parts", "wide"), None),
            P(("parts", "wide"), ("narrow", "sub"), None),
            P(("parts", "wide"), ("narrow", "sub"), None),
        ),
        out_specs=(
            P(("parts", "wide"), ("narrow", "sub"), None),
            P(("parts", "wide"), ("narrow", "sub"), None),
        ),
        check_vma=False,
    )
```

```python
import functools

import jax
import jax.numpy as jnp
from jax import lax
from jax.experimental import pallas as pl
from jax.experimental.pallas import tpu as pltpu
from jax.sharding import PartitionSpec as P

ROWT = 128
LANES = 128
GROUP = 8
TRIANGLE = ROWT // 2 + GROUP
PACKED = ROWT + 2 * TRIANGLE
MIB = 1024 * 1024

f32 = jnp.float32
bf16 = jnp.bfloat16


def split(x):
    high = x.astype(bf16)
    return high, (x - high.astype(f32)).astype(bf16)


def left(pair, axis):
    return jnp.concatenate([pair[0], pair[1], pair[0]], axis)


def right(pair, axis):
    return jnp.concatenate([pair[0], pair[0], pair[1]], axis)


def product(a, b, a_dim, b_dim):
    return lax.dot_general(a, b, (((a_dim,), (b_dim,)), ((), ())), preferred_element_type=f32)


def full_rows(tiles_ref, slot, blocks_ref, sub, row_tiles):
    tiles = tiles_ref.shape[2]
    rows = []
    for r in range(row_tiles):
        total = None
        for t in range(tiles):
            here = (blocks_ref[sub, slot, t] == r).astype(f32)
            term = tiles_ref[0, slot, t] * here
            total = term if total is None else total + term
        rows.append(total)
    return jnp.concatenate(rows, 0)


def contributions(phi, inverse, stiffs, masses):
    held = phi.shape[1]
    width = stiffs[0][0].shape[1]
    sides = [jnp.concatenate(x, 1) for x in zip(*stiffs, *masses, strict=True)]
    projected = product(left(split(phi.T), 1), right(sides, 0), 1, 0)
    scale = jnp.broadcast_to(inverse, (LANES, held)).T
    scale = jnp.concatenate([scale] * (width // LANES), 1)
    slots = len(stiffs)
    for slot in range(slots):
        p = projected[:, slot * width : (slot + 1) * width]
        q = projected[:, (slots + slot) * width : (slots + slot + 1) * width]
        first = scale * p
        second = scale * (0.5 * first - q)
        both = [jnp.concatenate(x, 1) for x in zip(split(first), split(second), strict=True)]
        yield product(left(split(p.T), 1), right(both, 0), 1, 0)


def local_kernel(start, has_acc, info, blocks, adjacency, modes_ref, eig_ref, stiff_ref, mass_ref, *refs):
    acc_in = refs[0] if has_acc else None
    s_ref, m_ref, acc_ref = refs[-3:]

    @pl.when(pl.program_id(0) == 0)
    def _():
        acc_ref[...] = acc_in[...] if has_acc else jnp.zeros_like(acc_ref)

    sub = pl.program_id(0) + start
    row_tiles = modes_ref.shape[0] // ROWT
    slots = stiff_ref.shape[1]
    stiffs, masses = [], []
    for slot in range(slots):
        for pairs, tiles_ref, pair_ref in ((stiffs, stiff_ref, s_ref), (masses, mass_ref, m_ref)):
            pairs.append(split(full_rows(tiles_ref, slot, blocks, sub, row_tiles)))
            pair_ref[0, slot, 0], pair_ref[0, slot, 1] = pairs[-1]
    inverse = 1.0 / eig_ref[pl.ds(sub, 1), :]
    for slot, update in enumerate(contributions(modes_ref[...], inverse, stiffs, masses)):
        acc_ref[adjacency[sub, info[0] * slots + slot]] += update


def whole(shape):
    return pl.BlockSpec(shape, functools.partial(lambda n, i: (0,) * n, len(shape)))


def once(shape):
    return pl.BlockSpec(
        shape, functools.partial(lambda n, i: (0,) * n, len(shape)), pipeline_mode=pl.Buffered(1)
    )


def params(limit):
    return pltpu.CompilerParams(vmem_limit_bytes=limit * MIB)


def cost(count, rows, held, slots, width):
    flops = 6 * count * 4 * slots * rows * held * width
    return pl.CostEstimate(flops=flops, bytes_accessed=count * 3 * MIB, transcendentals=0)


def local_sums(scalars, flat, eigvals, stiff, mass, start, count, limit, ifaces, acc=None):
    subs, slots, tiles, rowt, width = stiff.shape
    held = flat.shape[1]
    rows = flat.shape[0] // subs
    tile_spec = pl.BlockSpec((1, slots, tiles, rowt, width), lambda i: (i + start, 0, 0, 0, 0))
    pair_spec = pl.BlockSpec((1, slots, 2, rows, width), lambda i: (i, 0, 0, 0, 0))
    pair = jax.ShapeDtypeStruct((count, slots, 2, rows, width), bf16)
    shape = (ifaces, width, 2 * width)
    given = [] if acc is None else [acc]
    return pl.pallas_call(
        functools.partial(local_kernel, start, acc is not None),
        grid=(count,),
        in_specs=[pl.BlockSpec(memory_space=pltpu.SMEM)] * 3
        + [pl.BlockSpec((rows, held), lambda i: (i + start, 0)), whole(eigvals.shape), tile_spec, tile_spec]
        + [once(shape)] * len(given),
        out_specs=[pair_spec, pair_spec, whole(shape)],
        out_shape=[pair, pair, jax.ShapeDtypeStruct(shape, f32)],
        compiler_params=params(limit),
        cost_estimate=cost(count, rows, held, slots, width),
    )(*scalars, flat, eigvals, stiff, mass, *given)


def pairs_of(ref, place=0):
    return [(ref[place, slot, 0], ref[place, slot, 1]) for slot in range(ref.shape[1])]


def sum_kernel(start, info, adjacency, modes_ref, eig_ref, s_ref, m_ref, acc_in, acc_ref):
    @pl.when(pl.program_id(0) == 0)
    def _():
        acc_ref[...] = acc_in[...]

    sub = pl.program_id(0) + start
    slots = s_ref.shape[1]
    inverse = 1.0 / eig_ref[pl.ds(sub, 1), :]
    sums = contributions(modes_ref[...], inverse, pairs_of(s_ref), pairs_of(m_ref))
    for slot, update in enumerate(sums):
        acc_ref[adjacency[sub, info[0] * slots + slot]] += update


def pair_specs(pairs, offset):
    return [
        pl.BlockSpec((1, *pair.shape[1:]), lambda i: (i + offset, 0, 0, 0, 0)) for pair in pairs
    ]


def arrived_sums(scalars, modes, eigs, pairs, start, offset, count, acc):
    slots, _, rows, width = pairs[0].shape[1:]
    held = modes.shape[1]
    return pl.pallas_call(
        functools.partial(sum_kernel, start),
        grid=(count,),
        in_specs=[pl.BlockSpec(memory_space=pltpu.SMEM)] * 2
        + [pl.BlockSpec((rows, held), lambda i: (i, 0)), whole(eigs.shape)]
        + pair_specs(pairs, offset)
        + [once(acc.shape)],
        out_specs=whole(acc.shape),
        out_shape=jax.ShapeDtypeStruct(acc.shape, f32),
        compiler_params=params(24),
        cost_estimate=cost(count, rows, held, slots, width),
    )(*scalars, modes, eigs, *pairs, acc)


def folded(square):
    half = ROWT // 2
    row = lax.broadcasted_iota(jnp.int32, (half, ROWT), 0)
    col = lax.broadcasted_iota(jnp.int32, (half, ROWT), 1)
    top, bottom = square[:half], square[half:]
    diagonal = jnp.sum(jnp.where(row == col, top, 0.0), axis=0, keepdims=True)
    return jnp.where(col <= row + half, bottom, pltpu.roll(top, half, 1)), diagonal


def unfolded(part, diagonal):
    half = ROWT // 2
    row = lax.broadcasted_iota(jnp.int32, (half, ROWT), 0)
    col = lax.broadcasted_iota(jnp.int32, (half, ROWT), 1)
    bottom = jnp.where(col < row + half, part, 0.0)
    top = jnp.where((col > row) & (col < half), pltpu.roll(part, half, 1), 0.0)
    single = jnp.concatenate([top, bottom], 0)
    diagonals = [jnp.where(row == col, diagonal, 0.0), jnp.where(col == row + half, part, 0.0)]
    return single + single.T + jnp.concatenate(diagonals, 0)


def pack(sums):
    corners, firsts, seconds = [], [], []
    for which in range(2):
        base = which * 2 * ROWT
        first = sums(slice(0, ROWT), slice(base, base + ROWT))
        second = sums(slice(ROWT, 2 * ROWT), slice(base + ROWT, base + 2 * ROWT))
        corner = sums(slice(ROWT, 2 * ROWT), slice(base, base + ROWT))
        if which == 1:
            corner = corner + sums(slice(0, ROWT), slice(base + ROWT, base + 2 * ROWT)).T
            first, second = first + first.T, second + second.T
        corners.append(corner)
        firsts.append(folded(first))
        seconds.append(folded(second))
    triangles = []
    for squares in (firsts, seconds):
        parts, diagonals = (jnp.concatenate(x, 1) for x in zip(*squares, strict=True))
        triangles.append(
            jnp.concatenate([parts, jnp.broadcast_to(diagonals, (GROUP, 2 * ROWT))], 0)
        )
    return jnp.concatenate(corners, 1), *triangles


def places(side):
    first = pl.ds(pl.multiple_of(ROWT + (1 - side) * TRIANGLE, GROUP), TRIANGLE)
    second = pl.ds(pl.multiple_of(ROWT + side * TRIANGLE, GROUP), TRIANGLE)
    return pl.ds(0, ROWT), first, second


def pack_kernel(info, acc_ref, send_ref, keep_ref):
    side, chip, core = info[0], info[1], info[2]

    def one(shift, carry):
        target = lax.bitwise_xor(chip, shift) * 2
        for owner, out_ref in ((target + 1 - core, send_ref), (target + core, keep_ref)):
            parts = pack(lambda r, c, o=owner: acc_ref[o, r, c])
            for part, rows in zip(parts, places(side), strict=True):
                out_ref[shift, rows, :] = part
        return carry

    lax.fori_loop(0, send_ref.shape[0], one, 0)


def packed_sums(info, acc, shape):
    return pl.pallas_call(
        pack_kernel,
        in_specs=[pl.BlockSpec(memory_space=pltpu.SMEM), pl.BlockSpec(memory_space=pltpu.VMEM)],
        out_specs=[pl.BlockSpec(memory_space=pltpu.VMEM)] * 2,
        out_shape=[jax.ShapeDtypeStruct(shape, f32)] * 2,
        compiler_params=params(16),
        cost_estimate=pl.CostEstimate(flops=8_000_000, bytes_accessed=MIB, transcendentals=0),
    )(info, acc)


def add_kernel(
    sub, info, adjacency, modes_ref, eig_ref, s_ref, m_ref, send_in, keep_in, send_ref, keep_ref, held, sems
):
    side, chip, core = info[0], info[1], info[2]
    slots = s_ref.shape[1]

    def copies(slot, inward):
        owner = adjacency[sub, side * slots + slot]
        shift = lax.bitwise_xor(owner // 2, chip)
        mine = lax.rem(owner, 2) == core
        for here, ref in ((mine, keep_ref), (jnp.logical_not(mine), send_ref)):
            ends = (ref.at[shift], held.at[slot])
            source, target = ends if inward else ends[::-1]
            yield here, pltpu.make_async_copy(source, target, sems.at[slot])

    def run(slot, inward, wait):
        for here, copy in copies(slot, inward):

            @pl.when(here)
            def _(copy=copy):
                if wait:
                    copy.wait()
                else:
                    copy.start()

    for slot in range(slots):
        run(slot, True, False)
    inverse = 1.0 / eig_ref[sub : sub + 1, :]
    sums = contributions(modes_ref[...], inverse, pairs_of(s_ref), pairs_of(m_ref))
    for slot, update in enumerate(sums):
        parts = pack(lambda r, c, u=update: u[r, c])
        run(slot, True, True)
        for part, rows in zip(parts, places(side), strict=True):
            held[slot, rows, :] += part
        run(slot, False, False)
    for slot in range(slots):
        run(slot, False, True)


def added_sums(scalars, modes, eigs, pairs, sub, offset, sums):
    slots, _, rows, width = pairs[0].shape[1:]
    held = modes.shape[1]
    anywhere = pl.BlockSpec(memory_space=pl.ANY)
    return pl.pallas_call(
        functools.partial(add_kernel, sub),
        grid=(1,),
        in_specs=[pl.BlockSpec(memory_space=pltpu.SMEM)] * 2
        + [pl.BlockSpec((rows, held), lambda i: (i, 0)), whole(eigs.shape)]
        + pair_specs(pairs, offset)
        + [anywhere] * 2,
        out_specs=[anywhere] * 2,
        out_shape=[jax.ShapeDtypeStruct(x.shape, f32) for x in sums],
        scratch_shapes=[
            pltpu.VMEM((slots, *sums[0].shape[1:]), f32),
            pltpu.SemaphoreType.DMA((slots,)),
        ],
        input_output_aliases={6: 0, 7: 1},
        compiler_params=params(16),
        cost_estimate=cost(1, rows, held, slots, width),
    )(*scalars, modes, eigs, *pairs, *sums)


def unpack_kernel(info, mine, theirs, triangle_ref, stiff_ref, mass_ref, out_stiff, out_mass):
    side = info[0]
    half = ROWT // 2
    for which, (iface_ref, out_ref) in enumerate(((stiff_ref, out_stiff), (mass_ref, out_mass))):
        sign = -1.0 if which == 0 else 1.0
        lanes = slice(which * ROWT, (which + 1) * ROWT)
        corner = sign * (mine[:, lanes] + theirs[:, lanes])
        square = sign * unfolded(triangle_ref[:half, lanes], triangle_ref[half : half + 1, lanes])
        low, mid = slice(0, ROWT), slice(ROWT, 2 * ROWT)

        @pl.when(side == 0)
        def _():
            out_ref[0, :, low] = iface_ref[0, :, low] + square
            out_ref[0, :, mid] = iface_ref[0, :, mid] + corner.T

        @pl.when(side != 0)
        def _():
            out_ref[0, :, low] = iface_ref[0, :, low] + corner
            out_ref[0, :, mid] = iface_ref[0, :, mid] + square


def unpack(info, sums, iface_stiff, iface_mass):
    vmem = pl.BlockSpec(memory_space=pltpu.VMEM)
    return pl.pallas_call(
        unpack_kernel,
        in_specs=[pl.BlockSpec(memory_space=pltpu.SMEM)] + [vmem] * 5,
        out_specs=(vmem, vmem),
        out_shape=(jax.ShapeDtypeStruct(iface_stiff.shape, f32),) * 2,
        compiler_params=params(8),
    )(info, *sums, iface_stiff, iface_mass)


def paired(modes, eigvals, stiff, mass, blocks, adjacency, iface_stiff, iface_mass):
    subs, rows, held = modes.shape
    n_wide = lax.axis_size("wide")
    chips = n_wide // 2
    side, wide = lax.axis_index("narrow"), lax.axis_index("wide")
    info = jnp.stack([side, wide // 2, wide % 2]).astype(jnp.int32)
    flat = modes.reshape(subs * rows, held)

    def swap(x):
        return lax.ppermute(x, "narrow", [(0, 1), (1, 0)])

    def over_wide(x, mask):
        return lax.ppermute(x, "wide", [(i, i ^ mask) for i in range(n_wide)])

    def after(x, *others):
        return lax.optimization_barrier((x, *others))

    half = subs // 2
    cuts = [0, half, subs - 2, subs - 1, subs]
    pieces = [flat[a * rows : b * rows] for a, b in zip(cuts[:-1], cuts[1:], strict=True)]
    pieces[0], flat, eigvals, stiff, mass = after(pieces[0], flat, eigvals, stiff, mass)
    came = [swap(pieces[0])]
    local = functools.partial(local_sums, [info, blocks, adjacency], flat, eigvals, stiff, mass)
    *early, acc = local(0, half, 48, n_wide)
    sent, acc = after(eigvals, acc)
    eigs = swap(sent)
    *late, acc = local(half, subs - half, 48, n_wide, acc)
    sent, acc = after(pieces[1], acc)
    came.append(swap(sent))
    sent, came[0] = after(pieces[2], came[0])
    came.append(swap(sent))

    scalars = [info, adjacency]
    acc = arrived_sums(scalars, came[0], eigs, early, 0, 0, half, acc)
    sent, acc = after(pieces[3], acc)
    came.append(swap(sent))
    acc = arrived_sums(scalars, came[1], eigs, late, half, 0, cuts[2] - half, acc)
    sums = packed_sums(info, acc, (chips, PACKED, 2 * ROWT))
    for k in (2, 3):
        sums = added_sums(scalars, came[k], eigs, late, cuts[k], cuts[k] - half, sums)
    send, keep = sums

    def over_chips(x):
        parts = [over_wide(x[shift], 2 * shift) for shift in range(chips - 1, 0, -1)]
        return sum(parts, x[0])

    away, home = slice(ROWT, ROWT + TRIANGLE), slice(ROWT + TRIANGLE, PACKED)
    got = over_wide(send, 1)
    corners = keep[:, :ROWT] + got[:, :ROWT]
    corner = over_chips(corners)
    sent, corners = after(keep[:, away] + got[:, away], corners)
    came_away = swap(sent)
    corner_theirs = swap(corner)
    came_away, corner = after(came_away, corner)
    triangle = over_chips(keep[:, home] + got[:, home] + came_away)
    return unpack(info, (corner, corner_theirs, triangle), iface_stiff, iface_mass)


def grouped(modes, eigvals, stiff, mass, blocks, adjacency, iface_stiff, iface_mass):
    subs, rows, _ = modes.shape
    width = stiff.shape[4]
    n_wide = lax.axis_size("wide")
    info = jnp.stack([lax.axis_index("narrow")] * 3).astype(jnp.int32)
    modes = lax.all_gather(modes, "narrow", axis=2, tiled=True)
    eigvals = lax.all_gather(eigvals, "narrow", axis=1, tiled=True)
    flat = modes.reshape(subs * rows, modes.shape[2])
    _, _, acc = local_sums([info, blocks, adjacency], flat, eigvals, stiff, mass, 0, subs, 52, n_wide)
    half = acc[:, :, width:]
    part = jnp.concatenate([acc[:, :, :width], half + jnp.swapaxes(half, 1, 2)], 2)
    part = lax.psum_scatter(part, "wide", scatter_dimension=0, tiled=True)
    part = lax.psum_scatter(part, ("narrow", "sub"), scatter_dimension=1, tiled=True)
    return iface_stiff - part[:, :, :width], iface_mass + part[:, :, width:]


def solution(mesh):
    wide = mesh.shape["wide"]
    pairs = mesh.shape["narrow"] == 2 and mesh.shape["sub"] == 1 and wide > 1 and wide & (wide - 1) == 0
    return jax.shard_map(
        paired if pairs else grouped,
        mesh=mesh,
        in_specs=(
            P(("parts", "wide"), None, ("narrow", "sub")),
            P(("parts", "wide"), ("narrow", "sub")),
            P(("parts", "wide"), "narrow", None, None, None),
            P(("parts", "wide"), "narrow", None, None, None),
            P(("parts", "wide"), "narrow", None),
            P(("parts", "wide"), None),
            P(("parts", "wide"), ("narrow", "sub"), None),
            P(("parts", "wide"), ("narrow", "sub"), None),
        ),
        out_specs=(
            P(("parts", "wide"), ("narrow", "sub"), None),
            P(("parts", "wide"), ("narrow", "sub"), None),
        ),
        check_vma=False,
    )
```

```python
import functools

import jax
import jax.numpy as jnp
from jax import lax
from jax.experimental import pallas as pl
from jax.experimental.pallas import tpu as pltpu
from jax.sharding import PartitionSpec as P

ROWT = 128
LANES = 128
GROUP = 8
TRIANGLE = ROWT // 2 + GROUP
MIB = 1024 * 1024

f32 = jnp.float32
bf16 = jnp.bfloat16


def split(x):
    high = x.astype(bf16)
    return high, (x - high.astype(f32)).astype(bf16)


def left(pair, axis):
    return jnp.concatenate([pair[0], pair[1], pair[0]], axis)


def right(pair, axis):
    return jnp.concatenate([pair[0], pair[0], pair[1]], axis)


def product(a, b, a_dim, b_dim):
    return lax.dot_general(a, b, (((a_dim,), (b_dim,)), ((), ())), preferred_element_type=f32)


def full_rows(tiles_ref, slot, blocks_ref, sub, row_tiles):
    tiles = tiles_ref.shape[2]
    rows = []
    for r in range(row_tiles):
        total = None
        for t in range(tiles):
            here = (blocks_ref[sub, slot, t] == r).astype(f32)
            term = tiles_ref[0, slot, t] * here
            total = term if total is None else total + term
        rows.append(total)
    return jnp.concatenate(rows, 0)


def contributions(phi, inverse, stiffs, masses):
    held = phi.shape[1]
    width = stiffs[0][0].shape[1]
    sides = [jnp.concatenate(x, 1) for x in zip(*stiffs, *masses, strict=True)]
    projected = product(left(split(phi.T), 1), right(sides, 0), 1, 0)
    scale = jnp.broadcast_to(inverse, (LANES, held)).T
    scale = jnp.concatenate([scale] * (width // LANES), 1)
    slots = len(stiffs)
    for slot in range(slots):
        p = projected[:, slot * width : (slot + 1) * width]
        q = projected[:, (slots + slot) * width : (slots + slot + 1) * width]
        first = scale * p
        second = scale * (0.5 * first - q)
        both = [jnp.concatenate(x, 1) for x in zip(split(first), split(second), strict=True)]
        yield product(left(split(p.T), 1), right(both, 0), 1, 0)


def local_kernel(start, has_acc, info, blocks, adjacency, modes_ref, eig_ref, stiff_ref, mass_ref, *refs):
    acc_in = refs[0] if has_acc else None
    s_ref, m_ref, acc_ref = refs[-3:]

    @pl.when(pl.program_id(0) == 0)
    def _():
        acc_ref[...] = acc_in[...] if has_acc else jnp.zeros_like(acc_ref)

    sub = pl.program_id(0) + start
    row_tiles = modes_ref.shape[0] // ROWT
    slots = stiff_ref.shape[1]
    stiffs, masses = [], []
    for slot in range(slots):
        for pairs, tiles_ref, pair_ref in ((stiffs, stiff_ref, s_ref), (masses, mass_ref, m_ref)):
            pairs.append(split(full_rows(tiles_ref, slot, blocks, sub, row_tiles)))
            pair_ref[0, slot, 0], pair_ref[0, slot, 1] = pairs[-1]
    inverse = 1.0 / eig_ref[pl.ds(sub, 1), :]
    for slot, update in enumerate(contributions(modes_ref[...], inverse, stiffs, masses)):
        acc_ref[adjacency[sub, info[0] * slots + slot]] += update


def whole(shape):
    return pl.BlockSpec(shape, functools.partial(lambda n, i: (0,) * n, len(shape)))


def once(shape):
    return pl.BlockSpec(
        shape, functools.partial(lambda n, i: (0,) * n, len(shape)), pipeline_mode=pl.Buffered(1)
    )


def params(limit):
    return pltpu.CompilerParams(vmem_limit_bytes=limit * MIB)


def cost(count, rows, held, slots, width):
    flops = 6 * count * 4 * slots * rows * held * width
    return pl.CostEstimate(flops=flops, bytes_accessed=count * 3 * MIB, transcendentals=0)


def local_sums(scalars, flat, eigvals, stiff, mass, start, count, limit, ifaces, acc=None):
    subs, slots, tiles, rowt, width = stiff.shape
    held = flat.shape[1]
    rows = flat.shape[0] // subs
    tile_spec = pl.BlockSpec((1, slots, tiles, rowt, width), lambda i: (i + start, 0, 0, 0, 0))
    pair_spec = pl.BlockSpec((1, slots, 2, rows, width), lambda i: (i, 0, 0, 0, 0))
    pair = jax.ShapeDtypeStruct((count, slots, 2, rows, width), bf16)
    shape = (ifaces, width, 2 * width)
    given = [] if acc is None else [acc]
    return pl.pallas_call(
        functools.partial(local_kernel, start, acc is not None),
        grid=(count,),
        in_specs=[pl.BlockSpec(memory_space=pltpu.SMEM)] * 3
        + [pl.BlockSpec((rows, held), lambda i: (i + start, 0)), whole(eigvals.shape), tile_spec, tile_spec]
        + [once(shape)] * len(given),
        out_specs=[pair_spec, pair_spec, whole(shape)],
        out_shape=[pair, pair, jax.ShapeDtypeStruct(shape, f32)],
        compiler_params=params(limit),
        cost_estimate=pl.CostEstimate(flops=1000, bytes_accessed=1000, transcendentals=0),
    )(*scalars, flat, eigvals, stiff, mass, *given)


def pairs_of(ref, place=0):
    return [(ref[place, slot, 0], ref[place, slot, 1]) for slot in range(ref.shape[1])]


def sum_kernel(start, info, adjacency, modes_ref, eig_ref, s_ref, m_ref, acc_in, acc_ref):
    @pl.when(pl.program_id(0) == 0)
    def _():
        acc_ref[...] = acc_in[...]

    sub = pl.program_id(0) + start
    slots = s_ref.shape[1]
    inverse = 1.0 / eig_ref[pl.ds(sub, 1), :]
    sums = contributions(modes_ref[...], inverse, pairs_of(s_ref), pairs_of(m_ref))
    for slot, update in enumerate(sums):
        acc_ref[adjacency[sub, info[0] * slots + slot]] += update


def pair_specs(pairs, offset):
    return [
        pl.BlockSpec((1, *pair.shape[1:]), lambda i: (i + offset, 0, 0, 0, 0)) for pair in pairs
    ]


def arrived_sums(scalars, modes, eigs, pairs, start, offset, count, acc):
    slots, _, rows, width = pairs[0].shape[1:]
    held = modes.shape[1]
    return pl.pallas_call(
        functools.partial(sum_kernel, start),
        grid=(count,),
        in_specs=[pl.BlockSpec(memory_space=pltpu.SMEM)] * 2
        + [pl.BlockSpec((rows, held), lambda i: (i, 0)), whole(eigs.shape)]
        + pair_specs(pairs, offset)
        + [once(acc.shape)],
        out_specs=whole(acc.shape),
        out_shape=jax.ShapeDtypeStruct(acc.shape, f32),
        compiler_params=params(48),
        cost_estimate=cost(count, rows, held, slots, width),
    )(*scalars, modes, eigs, *pairs, acc)


def folded(square):
    half = ROWT // 2
    row = lax.broadcasted_iota(jnp.int32, (half, ROWT), 0)
    col = lax.broadcasted_iota(jnp.int32, (half, ROWT), 1)
    top, bottom = square[:half], square[half:]
    diagonal = jnp.sum(jnp.where(row == col, top, 0.0), axis=0, keepdims=True)
    return jnp.where(col <= row + half, bottom, pltpu.roll(top, half, 1)), diagonal


def unfolded(part, diagonal):
    half = ROWT // 2
    row = lax.broadcasted_iota(jnp.int32, (half, ROWT), 0)
    col = lax.broadcasted_iota(jnp.int32, (half, ROWT), 1)
    bottom = jnp.where(col < row + half, part, 0.0)
    top = jnp.where((col > row) & (col < half), pltpu.roll(part, half, 1), 0.0)
    single = jnp.concatenate([top, bottom], 0)
    diagonals = [jnp.where(row == col, diagonal, 0.0), jnp.where(col == row + half, part, 0.0)]
    return single + single.T + jnp.concatenate(diagonals, 0)


def pack(sums):
    corners, firsts, seconds = [], [], []
    for which in range(2):
        base = which * 2 * ROWT
        first = sums(slice(0, ROWT), slice(base, base + ROWT))
        second = sums(slice(ROWT, 2 * ROWT), slice(base + ROWT, base + 2 * ROWT))
        corner = sums(slice(ROWT, 2 * ROWT), slice(base, base + ROWT))
        if which == 1:
            corner = corner + sums(slice(0, ROWT), slice(base + ROWT, base + 2 * ROWT)).T
            first, second = first + first.T, second + second.T
        corners.append(corner)
        firsts.append(folded(first))
        seconds.append(folded(second))
    triangles = []
    for squares in (firsts, seconds):
        parts, diagonals = (jnp.concatenate(x, 1) for x in zip(*squares, strict=True))
        triangles.append(
            jnp.concatenate([parts, jnp.broadcast_to(diagonals, (GROUP, 2 * ROWT))], 0)
        )
    return jnp.concatenate(corners, 1), *triangles


def places(side):
    first = pl.ds(pl.multiple_of((1 - side) * TRIANGLE, GROUP), TRIANGLE)
    second = pl.ds(pl.multiple_of(side * TRIANGLE, GROUP), TRIANGLE)
    return first, second


def pack_kernel(info, acc_ref, send_corner, send_triangle, keep_corner, keep_triangle):
    side, chip, core = info[0], info[1], info[2]

    def one(shift, carry):
        target = lax.bitwise_xor(chip, shift) * 2
        for owner, corner_ref, triangle_ref in (
            (target + 1 - core, send_corner, send_triangle),
            (target + core, keep_corner, keep_triangle),
        ):
            corner, *triangles = pack(lambda r, c, o=owner: acc_ref[o, r, c])
            corner_ref[shift] = corner
            for triangle, rows in zip(triangles, places(side), strict=True):
                triangle_ref[shift, rows, :] = triangle
        return carry

    lax.fori_loop(0, send_corner.shape[0], one, 0)


def packed_sums(info, acc, shapes):
    return pl.pallas_call(
        pack_kernel,
        in_specs=[pl.BlockSpec(memory_space=pltpu.SMEM), pl.BlockSpec(memory_space=pltpu.VMEM)],
        out_specs=[pl.BlockSpec(memory_space=pltpu.VMEM)] * 4,
        out_shape=[jax.ShapeDtypeStruct(shape, f32) for shape in shapes * 2],
        compiler_params=params(16),
        cost_estimate=pl.CostEstimate(flops=8_000_000, bytes_accessed=MIB, transcendentals=0),
    )(info, acc)


def add_kernel(sub, lanes, modes_ref, eig_ref, s_ref, m_ref, owner_ref, side_ref, *refs):
    chips, slots = refs[0].shape[0], s_ref.shape[1]
    inverse = 1.0 / eig_ref[sub : sub + 1, lanes]
    sums = contributions(modes_ref[...], inverse, pairs_of(s_ref), pairs_of(m_ref))
    zero_side = side_ref[0:1, :] == 0.0
    corners, triangles = [], []
    for update in sums:
        corner, first, second = pack(lambda r, c, u=update: u[r, c])
        away, home = jnp.where(zero_side, second, first), jnp.where(zero_side, first, second)
        corners.append(corner)
        triangles.append(jnp.concatenate([away, home], 0))
    for k, packed in enumerate((corners, triangles, corners, triangles)):
        in_ref, out_ref = refs[k], refs[4 + k]
        for shift in range(chips):
            total = in_ref[shift]
            for slot in range(slots):
                row = slot * 2 * chips + k // 2 * chips + shift
                total = total + jnp.where(owner_ref[row : row + 1, :] > 0.0, packed[slot], 0.0)
            out_ref[shift] = total


def added_sums(modes, eigs, pairs, sub, offset, first, owners, side, sums):
    slots, _, rows, width = pairs[0].shape[1:]
    held = modes.shape[1]
    vmem = pl.BlockSpec(memory_space=pltpu.VMEM)
    return pl.pallas_call(
        functools.partial(add_kernel, sub, slice(first, first + held)),
        grid=(1,),
        in_specs=[vmem] * 2 + pair_specs(pairs, offset) + [vmem] * 6,
        out_specs=[vmem] * 4,
        out_shape=[jax.ShapeDtypeStruct(x.shape, f32) for x in sums],
        compiler_params=params(16),
        cost_estimate=cost(1, rows, held, slots, width),
    )(modes, eigs, *pairs, owners, side, *sums)


def unpack_kernel(side_ref, mine, theirs, triangle_ref, stiff_ref, mass_ref, out_stiff, out_mass):
    half = ROWT // 2
    zero_side = side_ref[0:1, :LANES] == 0.0
    low, mid = slice(0, ROWT), slice(ROWT, 2 * ROWT)
    for which, (iface_ref, out_ref) in enumerate(((stiff_ref, out_stiff), (mass_ref, out_mass))):
        sign = -1.0 if which == 0 else 1.0
        lanes = slice(which * ROWT, (which + 1) * ROWT)
        corner = sign * (mine[:, lanes] + theirs[:, lanes])
        square = sign * unfolded(triangle_ref[:half, lanes], triangle_ref[half : half + 1, lanes])
        out_ref[0, :, low] = iface_ref[0, :, low] + jnp.where(zero_side, square, corner)
        out_ref[0, :, mid] = iface_ref[0, :, mid] + jnp.where(zero_side, corner.T, square)


def unpack(side, sums, iface_stiff, iface_mass):
    vmem = pl.BlockSpec(memory_space=pltpu.VMEM)
    return pl.pallas_call(
        unpack_kernel,
        in_specs=[vmem] * 6,
        out_specs=(vmem, vmem),
        out_shape=(jax.ShapeDtypeStruct(iface_stiff.shape, f32),) * 2,
        compiler_params=params(8),
    )(side, *sums, iface_stiff, iface_mass)


def paired(modes, eigvals, stiff, mass, blocks, adjacency, iface_stiff, iface_mass):
    subs, rows, held = modes.shape
    n_wide = lax.axis_size("wide")
    chips = n_wide // 2
    side, wide = lax.axis_index("narrow"), lax.axis_index("wide")
    info = jnp.stack([side, wide // 2, wide % 2]).astype(jnp.int32)
    flat = modes.reshape(subs * rows, held)

    def swap(x):
        return lax.ppermute(x, "narrow", [(0, 1), (1, 0)])

    def over_wide(x, mask):
        return lax.ppermute(x, "wide", [(i, i ^ mask) for i in range(n_wide)])

    def after(x, *others):
        return lax.optimization_barrier((x, *others))

    half = subs // 2
    cuts = [0, half, subs - 2, subs - 1]
    pieces = [flat[a * rows : b * rows] for a, b in zip(cuts[:-1], cuts[1:], strict=True)]
    middle = held // 2 if False and held % (2 * LANES) == 0 else held
    last = flat[(subs - 1) * rows :]
    pieces += [last[:, lane : lane + middle] for lane in range(0, held, middle)]
    pieces[0], flat, eigvals, stiff, mass = after(pieces[0], flat, eigvals, stiff, mass)
    came = [swap(pieces[0])]
    local = functools.partial(local_sums, [info, blocks, adjacency], flat, eigvals, stiff, mass)
    *pairs, acc = local(0, subs, 52, n_wide)
    sent, own, acc = after(pieces[1], eigvals, acc)
    eigs = swap(own)
    came.append(swap(sent))
    slots = stiff.shape[1]
    chip, core = wide // 2, wide % 2
    targets = (chip ^ jnp.arange(chips)) * 2
    targets = jnp.concatenate([targets + 1 - core, targets + core])
    mine = lax.dynamic_slice_in_dim(adjacency, side * slots, slots, 1)[cuts[2] :]
    owners = (mine[:, :, None] == targets).astype(f32).reshape(-1, slots * 2 * chips, 1)
    owners = jnp.broadcast_to(owners, (*owners.shape[:2], 2 * ROWT))
    side_rows = jnp.full((GROUP, 2 * ROWT), side, f32)
    sent, came[0], owners, side_rows = after(pieces[2], came[0], owners, side_rows)
    came.append(swap(sent))

    scalars = [info, adjacency]
    lasts = [x[cuts[2] :] for x in pairs]
    acc = arrived_sums(scalars, came[0], eigs, pairs, 0, 0, half, acc)
    sent, acc = after(pieces[3], acc)
    came.append(swap(sent))
    acc = arrived_sums(scalars, came[1], eigs, pairs, half, half, cuts[2] - half, acc)
    for piece in pieces[4:]:
        sent, acc = after(piece, acc)
        came.append(swap(sent))
    sums = packed_sums(info, acc, [(chips, ROWT, 2 * ROWT), (chips, 2 * TRIANGLE, 2 * ROWT)])
    singles = [(subs - 2, 0)] + [(subs - 1, lane) for lane in range(0, held, middle)]
    for (sub, lane), modes_ in zip(singles, came[2:], strict=True):
        sums = added_sums(
            modes_, eigs, lasts, sub, sub - cuts[2], lane, owners[sub - cuts[2]], side_rows, sums
        )
    send_corner, send_triangle, keep_corner, keep_triangle = sums

    def over_chips(x):
        parts = [over_wide(x[shift], 2 * shift) for shift in range(chips - 1, 0, -1)]
        return sum(parts, x[0])

    away, home = slice(0, TRIANGLE), slice(TRIANGLE, 2 * TRIANGLE)
    corners = keep_corner + over_wide(send_corner, 1)
    got = over_wide(send_triangle, 1)
    corner = over_chips(corners)
    sent, corners = after(keep_triangle[:, away] + got[:, away], corners)
    came_away = swap(sent)
    corner_theirs = swap(corner)
    came_away, corner = after(came_away, corner)
    triangle = over_chips(keep_triangle[:, home] + got[:, home] + came_away)
    return unpack(side_rows, (corner, corner_theirs, triangle), iface_stiff, iface_mass)


def grouped(modes, eigvals, stiff, mass, blocks, adjacency, iface_stiff, iface_mass):
    subs, rows, _ = modes.shape
    width = stiff.shape[4]
    n_wide = lax.axis_size("wide")
    info = jnp.stack([lax.axis_index("narrow")] * 3).astype(jnp.int32)
    modes = lax.all_gather(modes, "narrow", axis=2, tiled=True)
    eigvals = lax.all_gather(eigvals, "narrow", axis=1, tiled=True)
    flat = modes.reshape(subs * rows, modes.shape[2])
    _, _, acc = local_sums([info, blocks, adjacency], flat, eigvals, stiff, mass, 0, subs, 52, n_wide)
    half = acc[:, :, width:]
    part = jnp.concatenate([acc[:, :, :width], half + jnp.swapaxes(half, 1, 2)], 2)
    part = lax.psum_scatter(part, "wide", scatter_dimension=0, tiled=True)
    part = lax.psum_scatter(part, ("narrow", "sub"), scatter_dimension=1, tiled=True)
    return iface_stiff - part[:, :, :width], iface_mass + part[:, :, width:]


def solution(mesh):
    wide = mesh.shape["wide"]
    pairs = mesh.shape["narrow"] == 2 and mesh.shape["sub"] == 1 and wide > 1 and wide & (wide - 1) == 0
    return jax.shard_map(
        paired if pairs else grouped,
        mesh=mesh,
        in_specs=(
            P(("parts", "wide"), None, ("narrow", "sub")),
            P(("parts", "wide"), ("narrow", "sub")),
            P(("parts", "wide"), "narrow", None, None, None),
            P(("parts", "wide"), "narrow", None, None, None),
            P(("parts", "wide"), "narrow", None),
            P(("parts", "wide"), None),
            P(("parts", "wide"), ("narrow", "sub"), None),
            P(("parts", "wide"), ("narrow", "sub"), None),
        ),
        out_specs=(
            P(("parts", "wide"), ("narrow", "sub"), None),
            P(("parts", "wide"), ("narrow", "sub"), None),
        ),
        check_vma=False,
    )
```

```python
import functools

import jax
import jax.numpy as jnp
from jax import lax
from jax.experimental import pallas as pl
from jax.experimental.pallas import tpu as pltpu
from jax.sharding import PartitionSpec as P

ROWT = 128
LANES = 128
GROUP = 8
TRIANGLE = ROWT // 2 + GROUP
MIB = 1024 * 1024

f32 = jnp.float32
bf16 = jnp.bfloat16


def split(x):
    high = x.astype(bf16)
    return high, (x - high.astype(f32)).astype(bf16)


def left(pair, axis):
    return jnp.concatenate([pair[0], pair[1], pair[0]], axis)


def right(pair, axis):
    return jnp.concatenate([pair[0], pair[0], pair[1]], axis)


def product(a, b, a_dim, b_dim):
    return lax.dot_general(a, b, (((a_dim,), (b_dim,)), ((), ())), preferred_element_type=f32)


def full_rows(tiles_ref, slot, blocks_ref, sub, row_tiles):
    tiles = tiles_ref.shape[2]
    rows = []
    for r in range(row_tiles):
        total = None
        for t in range(tiles):
            here = (blocks_ref[sub, slot, t] == r).astype(f32)
            term = tiles_ref[0, slot, t] * here
            total = term if total is None else total + term
        rows.append(total)
    return jnp.concatenate(rows, 0)


def contributions(phi, inverse, stiffs, masses):
    held = phi.shape[1]
    width = stiffs[0][0].shape[1]
    sides = [jnp.concatenate(x, 1) for x in zip(*stiffs, *masses, strict=True)]
    projected = product(left(split(phi.T), 1), right(sides, 0), 1, 0)
    scale = jnp.broadcast_to(inverse, (LANES, held)).T
    scale = jnp.concatenate([scale] * (width // LANES), 1)
    slots = len(stiffs)
    for slot in range(slots):
        p = projected[:, slot * width : (slot + 1) * width]
        q = projected[:, (slots + slot) * width : (slots + slot + 1) * width]
        first = scale * p
        second = scale * (0.5 * first - q)
        both = [jnp.concatenate(x, 1) for x in zip(split(first), split(second), strict=True)]
        yield product(left(split(p.T), 1), right(both, 0), 1, 0)


def local_kernel(start, has_acc, info, blocks, adjacency, modes_ref, eig_ref, stiff_ref, mass_ref, *refs):
    acc_in = refs[0] if has_acc else None
    s_ref, m_ref, acc_ref = refs[-3:]

    @pl.when(pl.program_id(0) == 0)
    def _():
        acc_ref[...] = acc_in[...] if has_acc else jnp.zeros_like(acc_ref)

    sub = pl.program_id(0) + start
    row_tiles = modes_ref.shape[0] // ROWT
    slots = stiff_ref.shape[1]
    stiffs, masses = [], []
    for slot in range(slots):
        for pairs, tiles_ref, pair_ref in ((stiffs, stiff_ref, s_ref), (masses, mass_ref, m_ref)):
            pairs.append(split(full_rows(tiles_ref, slot, blocks, sub, row_tiles)))
            pair_ref[0, slot, 0], pair_ref[0, slot, 1] = pairs[-1]
    inverse = 1.0 / eig_ref[pl.ds(sub, 1), :]
    for slot, update in enumerate(contributions(modes_ref[...], inverse, stiffs, masses)):
        acc_ref[adjacency[sub, info[0] * slots + slot]] += update


def whole(shape):
    return pl.BlockSpec(shape, functools.partial(lambda n, i: (0,) * n, len(shape)))


def once(shape):
    return pl.BlockSpec(
        shape, functools.partial(lambda n, i: (0,) * n, len(shape)), pipeline_mode=pl.Buffered(1)
    )


def params(limit):
    return pltpu.CompilerParams(vmem_limit_bytes=limit * MIB)


def cost(count, rows, held, slots, width):
    flops = 6 * count * 4 * slots * rows * held * width
    return pl.CostEstimate(flops=flops, bytes_accessed=count * 3 * MIB, transcendentals=0)


def local_sums(scalars, flat, eigvals, stiff, mass, start, count, limit, ifaces, acc=None):
    subs, slots, tiles, rowt, width = stiff.shape
    held = flat.shape[1]
    rows = flat.shape[0] // subs
    tile_spec = pl.BlockSpec((1, slots, tiles, rowt, width), lambda i: (i + start, 0, 0, 0, 0))
    pair_spec = pl.BlockSpec((1, slots, 2, rows, width), lambda i: (i, 0, 0, 0, 0))
    pair = jax.ShapeDtypeStruct((count, slots, 2, rows, width), bf16)
    shape = (ifaces, width, 2 * width)
    given = [] if acc is None else [acc]
    return pl.pallas_call(
        functools.partial(local_kernel, start, acc is not None),
        grid=(count,),
        in_specs=[pl.BlockSpec(memory_space=pltpu.SMEM)] * 3
        + [pl.BlockSpec((rows, held), lambda i: (i + start, 0)), whole(eigvals.shape), tile_spec, tile_spec]
        + [once(shape)] * len(given),
        out_specs=[pair_spec, pair_spec, whole(shape)],
        out_shape=[pair, pair, jax.ShapeDtypeStruct(shape, f32)],
        compiler_params=params(limit),
        cost_estimate=pl.CostEstimate(flops=1000, bytes_accessed=1000, transcendentals=0),
    )(*scalars, flat, eigvals, stiff, mass, *given)


def pairs_of(ref, place=0):
    return [(ref[place, slot, 0], ref[place, slot, 1]) for slot in range(ref.shape[1])]


def sum_kernel(start, info, adjacency, modes_ref, eig_ref, s_ref, m_ref, acc_in, acc_ref):
    @pl.when(pl.program_id(0) == 0)
    def _():
        acc_ref[...] = acc_in[...]

    sub = pl.program_id(0) + start
    slots = s_ref.shape[1]
    inverse = 1.0 / eig_ref[pl.ds(sub, 1), :]
    sums = contributions(modes_ref[...], inverse, pairs_of(s_ref), pairs_of(m_ref))
    for slot, update in enumerate(sums):
        acc_ref[adjacency[sub, info[0] * slots + slot]] += update


def pair_specs(pairs, offset):
    return [
        pl.BlockSpec((1, *pair.shape[1:]), lambda i: (i + offset, 0, 0, 0, 0)) for pair in pairs
    ]


def arrived_sums(scalars, modes, eigs, pairs, start, offset, count, acc):
    slots, _, rows, width = pairs[0].shape[1:]
    held = modes.shape[1]
    return pl.pallas_call(
        functools.partial(sum_kernel, start),
        grid=(count,),
        in_specs=[pl.BlockSpec(memory_space=pltpu.SMEM)] * 2
        + [pl.BlockSpec((rows, held), lambda i: (i, 0)), whole(eigs.shape)]
        + pair_specs(pairs, offset)
        + [once(acc.shape)],
        out_specs=whole(acc.shape),
        out_shape=jax.ShapeDtypeStruct(acc.shape, f32),
        compiler_params=params(48),
        cost_estimate=cost(count, rows, held, slots, width),
    )(*scalars, modes, eigs, *pairs, acc)


def folded(square):
    half = ROWT // 2
    row = lax.broadcasted_iota(jnp.int32, (half, ROWT), 0)
    col = lax.broadcasted_iota(jnp.int32, (half, ROWT), 1)
    top, bottom = square[:half], square[half:]
    diagonal = jnp.sum(jnp.where(row == col, top, 0.0), axis=0, keepdims=True)
    return jnp.where(col <= row + half, bottom, pltpu.roll(top, half, 1)), diagonal


def unfolded(part, diagonal):
    half = ROWT // 2
    row = lax.broadcasted_iota(jnp.int32, (half, ROWT), 0)
    col = lax.broadcasted_iota(jnp.int32, (half, ROWT), 1)
    bottom = jnp.where(col < row + half, part, 0.0)
    top = jnp.where((col > row) & (col < half), pltpu.roll(part, half, 1), 0.0)
    single = jnp.concatenate([top, bottom], 0)
    diagonals = [jnp.where(row == col, diagonal, 0.0), jnp.where(col == row + half, part, 0.0)]
    return single + single.T + jnp.concatenate(diagonals, 0)


def pack(sums):
    corners, firsts, seconds = [], [], []
    for which in range(2):
        base = which * 2 * ROWT
        first = sums(slice(0, ROWT), slice(base, base + ROWT))
        second = sums(slice(ROWT, 2 * ROWT), slice(base + ROWT, base + 2 * ROWT))
        corner = sums(slice(ROWT, 2 * ROWT), slice(base, base + ROWT))
        if which == 1:
            corner = corner + sums(slice(0, ROWT), slice(base + ROWT, base + 2 * ROWT)).T
            first, second = first + first.T, second + second.T
        corners.append(corner)
        firsts.append(folded(first))
        seconds.append(folded(second))
    triangles = []
    for squares in (firsts, seconds):
        parts, diagonals = (jnp.concatenate(x, 1) for x in zip(*squares, strict=True))
        triangles.append(
            jnp.concatenate([parts, jnp.broadcast_to(diagonals, (GROUP, 2 * ROWT))], 0)
        )
    return jnp.concatenate(corners, 1), *triangles


def places(side):
    first = pl.ds(pl.multiple_of((1 - side) * TRIANGLE, GROUP), TRIANGLE)
    second = pl.ds(pl.multiple_of(side * TRIANGLE, GROUP), TRIANGLE)
    return first, second


def pack_kernel(info, acc_ref, send_corner, send_triangle, keep_corner, keep_triangle):
    side, chip, core = info[0], info[1], info[2]

    def one(shift, carry):
        target = lax.bitwise_xor(chip, shift) * 2
        for owner, corner_ref, triangle_ref in (
            (target + 1 - core, send_corner, send_triangle),
            (target + core, keep_corner, keep_triangle),
        ):
            corner, *triangles = pack(lambda r, c, o=owner: acc_ref[o, r, c])
            corner_ref[shift] = corner
            for triangle, rows in zip(triangles, places(side), strict=True):
                triangle_ref[shift, rows, :] = triangle
        return carry

    lax.fori_loop(0, send_corner.shape[0], one, 0)


def packed_sums(info, acc, shapes):
    return pl.pallas_call(
        pack_kernel,
        in_specs=[pl.BlockSpec(memory_space=pltpu.SMEM), pl.BlockSpec(memory_space=pltpu.VMEM)],
        out_specs=[pl.BlockSpec(memory_space=pltpu.VMEM)] * 4,
        out_shape=[jax.ShapeDtypeStruct(shape, f32) for shape in shapes * 2],
        compiler_params=params(16),
        cost_estimate=pl.CostEstimate(flops=8_000_000, bytes_accessed=MIB, transcendentals=0),
    )(info, acc)


def add_kernel(sub, lanes, modes_ref, eig_ref, s_ref, m_ref, owner_ref, side_ref, *refs):
    chips, slots = refs[0].shape[0], s_ref.shape[1]
    inverse = 1.0 / eig_ref[sub : sub + 1, lanes]
    sums = contributions(modes_ref[...], inverse, pairs_of(s_ref), pairs_of(m_ref))
    zero_side = side_ref[0:1, :] == 0.0
    corners, triangles = [], []
    for update in sums:
        corner, first, second = pack(lambda r, c, u=update: u[r, c])
        away, home = jnp.where(zero_side, second, first), jnp.where(zero_side, first, second)
        corners.append(corner)
        triangles.append(jnp.concatenate([away, home], 0))
    for k, packed in enumerate((corners, triangles, corners, triangles)):
        in_ref, out_ref = refs[k], refs[4 + k]
        for shift in range(chips):
            total = in_ref[shift]
            for slot in range(slots):
                row = slot * 2 * chips + k // 2 * chips + shift
                total = total + jnp.where(owner_ref[row : row + 1, :] > 0.0, packed[slot], 0.0)
            out_ref[shift] = total


def added_sums(modes, eigs, pairs, sub, offset, first, owners, side, sums):
    slots, _, rows, width = pairs[0].shape[1:]
    held = modes.shape[1]
    vmem = pl.BlockSpec(memory_space=pltpu.VMEM)
    return pl.pallas_call(
        functools.partial(add_kernel, sub, slice(first, first + held)),
        grid=(1,),
        in_specs=[vmem] * 2 + pair_specs(pairs, offset) + [vmem] * 6,
        out_specs=[vmem] * 4,
        out_shape=[jax.ShapeDtypeStruct(x.shape, f32) for x in sums],
        compiler_params=params(16),
        cost_estimate=cost(1, rows, held, slots, width),
    )(modes, eigs, *pairs, owners, side, *sums)


def unpack_kernel(side_ref, mine, theirs, triangle_ref, stiff_ref, mass_ref, out_stiff, out_mass):
    half = ROWT // 2
    zero_side = side_ref[0:1, :LANES] == 0.0
    low, mid = slice(0, ROWT), slice(ROWT, 2 * ROWT)
    for which, (iface_ref, out_ref) in enumerate(((stiff_ref, out_stiff), (mass_ref, out_mass))):
        sign = -1.0 if which == 0 else 1.0
        lanes = slice(which * ROWT, (which + 1) * ROWT)
        corner = sign * (mine[:, lanes] + theirs[:, lanes])
        square = sign * unfolded(triangle_ref[:half, lanes], triangle_ref[half : half + 1, lanes])
        out_ref[0, :, low] = iface_ref[0, :, low] + jnp.where(zero_side, square, corner)
        out_ref[0, :, mid] = iface_ref[0, :, mid] + jnp.where(zero_side, corner.T, square)


def unpack(side, sums, iface_stiff, iface_mass):
    vmem = pl.BlockSpec(memory_space=pltpu.VMEM)
    return pl.pallas_call(
        unpack_kernel,
        in_specs=[vmem] * 6,
        out_specs=(vmem, vmem),
        out_shape=(jax.ShapeDtypeStruct(iface_stiff.shape, f32),) * 2,
        compiler_params=params(8),
    )(side, *sums, iface_stiff, iface_mass)


def paired(modes, eigvals, stiff, mass, blocks, adjacency, iface_stiff, iface_mass):
    subs, rows, held = modes.shape
    n_wide = lax.axis_size("wide")
    chips = n_wide // 2
    side, wide = lax.axis_index("narrow"), lax.axis_index("wide")
    info = jnp.stack([side, wide // 2, wide % 2]).astype(jnp.int32)
    flat = modes.reshape(subs * rows, held)

    def swap(x):
        return lax.ppermute(x, "narrow", [(0, 1), (1, 0)])

    def over_wide(x, mask):
        return lax.ppermute(x, "wide", [(i, i ^ mask) for i in range(n_wide)])

    def after(x, *others):
        return lax.optimization_barrier((x, *others))

    half = subs // 2
    cuts = [0, half, subs - 2, subs - 1]
    pieces = [flat[a * rows : b * rows] for a, b in zip(cuts[:-1], cuts[1:], strict=True)]
    middle = held // 2 if False and held % (2 * LANES) == 0 else held
    last = flat[(subs - 1) * rows :]
    pieces += [last[:, lane : lane + middle] for lane in range(0, held, middle)]
    pieces[0], flat, eigvals, stiff, mass = after(pieces[0], flat, eigvals, stiff, mass)
    came = [swap(pieces[0])]
    local = functools.partial(local_sums, [info, blocks, adjacency], flat, eigvals, stiff, mass)
    *pairs, acc = local(0, subs, 52, n_wide)
    sent, own, acc = after(pieces[1], eigvals, acc)
    eigs = swap(own)
    came.append(swap(sent))
    slots = stiff.shape[1]
    chip, core = wide // 2, wide % 2
    targets = (chip ^ jnp.arange(chips)) * 2
    targets = jnp.concatenate([targets + 1 - core, targets + core])
    mine = lax.dynamic_slice_in_dim(adjacency, side * slots, slots, 1)[cuts[2] :]
    owners = (mine[:, :, None] == targets).astype(f32).reshape(-1, slots * 2 * chips, 1)
    owners = jnp.broadcast_to(owners, (*owners.shape[:2], 2 * ROWT))
    side_rows = jnp.full((GROUP, 2 * ROWT), side, f32)
    sent, came[0], owners, side_rows = after(pieces[2], came[0], owners, side_rows)
    came.append(swap(sent))

    scalars = [info, adjacency]
    lasts = [x[cuts[2] :] for x in pairs]
    acc = arrived_sums(scalars, came[0], eigs, pairs, 0, 0, half, acc)
    sent, acc = after(pieces[3], acc)
    came.append(swap(sent))
    acc = arrived_sums(scalars, came[1], eigs, pairs, half, half, cuts[2] - half, acc)
    for piece in pieces[4:]:
        sent, acc = after(piece, acc)
        came.append(swap(sent))
    sums = packed_sums(info, acc, [(chips, ROWT, 2 * ROWT), (chips, 2 * TRIANGLE, 2 * ROWT)])
    singles = [(subs - 2, 0)] + [(subs - 1, lane) for lane in range(0, held, middle)]
    for (sub, lane), modes_ in zip(singles, came[2:], strict=True):
        sums = added_sums(
            modes_, eigs, lasts, sub, sub - cuts[2], lane, owners[sub - cuts[2]], side_rows, sums
        )
    send_corner, send_triangle, keep_corner, keep_triangle = sums

    def over_chips(x, order):
        parts = [over_wide(x[shift], 2 * shift) for shift in order]
        return sum(parts, x[0])

    away, home = slice(0, TRIANGLE), slice(TRIANGLE, 2 * TRIANGLE)
    corners = keep_corner + over_wide(send_corner, 1)
    got = over_wide(send_triangle, 1)
    corner = over_chips(corners, (2, 3, 1))
    sent, corners = after(keep_triangle[:, away] + got[:, away], corners)
    came_away = swap(sent)
    corner_theirs = swap(corner)
    came_away, corner = after(came_away, corner)
    triangle = over_chips(keep_triangle[:, home] + got[:, home] + came_away, (3, 2, 1))
    return unpack(side_rows, (corner, corner_theirs, triangle), iface_stiff, iface_mass)


def grouped(modes, eigvals, stiff, mass, blocks, adjacency, iface_stiff, iface_mass):
    subs, rows, _ = modes.shape
    width = stiff.shape[4]
    n_wide = lax.axis_size("wide")
    info = jnp.stack([lax.axis_index("narrow")] * 3).astype(jnp.int32)
    modes = lax.all_gather(modes, "narrow", axis=2, tiled=True)
    eigvals = lax.all_gather(eigvals, "narrow", axis=1, tiled=True)
    flat = modes.reshape(subs * rows, modes.shape[2])
    _, _, acc = local_sums([info, blocks, adjacency], flat, eigvals, stiff, mass, 0, subs, 52, n_wide)
    half = acc[:, :, width:]
    part = jnp.concatenate([acc[:, :, :width], half + jnp.swapaxes(half, 1, 2)], 2)
    part = lax.psum_scatter(part, "wide", scatter_dimension=0, tiled=True)
    part = lax.psum_scatter(part, ("narrow", "sub"), scatter_dimension=1, tiled=True)
    return iface_stiff - part[:, :, :width], iface_mass + part[:, :, width:]


def solution(mesh):
    wide = mesh.shape["wide"]
    pairs = mesh.shape["narrow"] == 2 and mesh.shape["sub"] == 1 and wide > 1 and wide & (wide - 1) == 0
    return jax.shard_map(
        paired if pairs else grouped,
        mesh=mesh,
        in_specs=(
            P(("parts", "wide"), None, ("narrow", "sub")),
            P(("parts", "wide"), ("narrow", "sub")),
            P(("parts", "wide"), "narrow", None, None, None),
            P(("parts", "wide"), "narrow", None, None, None),
            P(("parts", "wide"), "narrow", None),
            P(("parts", "wide"), None),
            P(("parts", "wide"), ("narrow", "sub"), None),
            P(("parts", "wide"), ("narrow", "sub"), None),
        ),
        out_specs=(
            P(("parts", "wide"), ("narrow", "sub"), None),
            P(("parts", "wide"), ("narrow", "sub"), None),
        ),
        check_vma=False,
    )
```
